256 devices in a mesh: gx: 16 (over x, z_lo), gy: 16 (over y, z_hi, core).
Axes of the slice: x: 4, y: 4, z: 8 (z_hi: 2, z_lo: 4; z = z_hi * 4 + z_lo), core: 2. Of those that a mesh axis runs over, the one named last changes fastest.
Arguments:
- images: float32 [1024, 128, 2048], P(None, 'gx', 'gy'), may hold values from 0 to 600, as said below
Outputs:
- colocal: float32 [1024, 1024], P(('gx', 'gy'))
The draws below stay inside these ranges and needn't reach their ends.
Inputs may be any that keep to these rules, and one draw needn't show every extreme that they name: `images`: intensities are non-negative.
All inputs are finite; a program needn't handle non-finite values.
Results may differ from the reference program's by a relative error of at most 0.00035.
Values sent between devices are 32-bit elements; how exact they have to be, the bound alone decides.
No kernel may reach another device: no remote copies, remote signals or barrier semaphores. Data moves between devices by JAX's collectives and lax.ppermute only.
A program may use at most 128 MiB of HBM per device.

```python
import math
import jax
import jax.numpy as jnp
from jax import lax

IMAGES = 1024
CH = 8
CW = 128
HEIGHT = 128
WIDTH = 2048


def draw_images(key, part):
    key = jax.random.fold_in(key, 11)
    keys = jax.random.split(key, 5)
    noise = jnp.clip(jax.random.normal(keys[0], (IMAGES, HEIGHT, WIDTH), jnp.float32), -4.0, 4.0)
    rough = jnp.exp(0.8 * noise)
    scale = jnp.exp(jax.random.uniform(keys[1], (IMAGES, 1, 1), jnp.float32) * 2.3)
    height_plateau = 4.0
    shared = jax.random.uniform(keys[2], (1, HEIGHT, WIDTH), jnp.float32, 0.5, 1.5)
    row_block = jax.random.randint(keys[3], (IMAGES,), 0, HEIGHT // CH)
    col_block = jax.random.randint(keys[4], (IMAGES,), 0, WIDTH // CW)
    row_ids = jnp.arange(HEIGHT, dtype=jnp.int32) // CH
    col_ids = jnp.arange(WIDTH, dtype=jnp.int32) // CW
    inside = (row_ids[None, :, None] == row_block[:, None, None]) & (col_ids[None, None, :] == col_block[:, None, None])
    plateau = jnp.where(inside, height_plateau * shared, 0.0)
    return (scale * (rough + plateau)).astype(jnp.float32)


def setup_inputs(seed: int = 0) -> dict:
    seeds = jax.random.split(jax.random.key(seed), 2)
    return {
        "images": draw_images(jax.random.fold_in(seeds[1], 71), 0),
    }


sigma_sq = 2.25

def stencil_taps():
    raw = [math.exp(-k * k / (2.0 * sigma_sq)) for k in range(-4, 5)]
    total = sum(raw)
    return [value / total for value in raw]

def smooth_block(block):
    taps = stencil_taps()
    rows_total = block.shape[1]
    cols_total = block.shape[2]
    padded = jnp.pad(block, ((0, 0), (4, 4), (0, 0)))
    vertical = taps[0] * padded[:, 0:rows_total, :]
    for k in range(1, 9):
        vertical = vertical + taps[k] * padded[:, k:k + rows_total, :]
    padded = jnp.pad(vertical, ((0, 0), (0, 0), (4, 4)))
    smooth = taps[0] * padded[:, :, 0:cols_total]
    for k in range(1, 9):
        smooth = smooth + taps[k] * padded[:, :, k:k + cols_total]
    count = jnp.float32(rows_total * cols_total)
    mean = lax.optimization_barrier(jnp.sum(smooth, axis=(1, 2))) / count
    centered = smooth - mean[:, None, None]
    spread = lax.optimization_barrier(jnp.sum(centered * centered, axis=(1, 2)))
    scale = 1.0 / jnp.sqrt(spread + 1e-06)
    unit = (centered * scale[:, None, None]).astype(jnp.bfloat16)
    return unit.reshape(block.shape[0], -1)

def reference(images):
    blocks = images.reshape(IMAGES // 64, 64, HEIGHT, WIDTH)
    unit = lax.map(smooth_block, blocks).reshape(IMAGES, HEIGHT * WIDTH)
    wide = unit.astype(jnp.float32)

    def gram_rows(rows):
        return jnp.dot(rows, wide.T, precision=lax.Precision.HIGHEST, preferred_element_type=jnp.float32)
    parts = lax.map(gram_rows, wide.reshape(IMAGES // 64, 64, HEIGHT * WIDTH))
    return parts.reshape(IMAGES, IMAGES)
```

```python
import math

import jax
import jax.numpy as jnp
import numpy as np
from jax import lax
from jax.experimental import pallas as pl
from jax.experimental.pallas import tpu as pltpu
from jax.sharding import Mesh, PartitionSpec as P

f32 = jnp.float32
HI = lax.Precision.HIGHEST
NT = (((1,), (1,)), ((), ()))
PIXELS = 128 * 2048


def stencil_taps():
    raw = [math.exp(-k * k / 4.5) for k in range(-4, 5)]
    total = sum(raw)
    return [value / total for value in raw]


TAPS = stencil_taps()


def edge_weights(length):
    weights = np.zeros(length, np.float64)
    for k in range(-4, 5):
        for out in range(length):
            if 0 <= out + k < length:
                weights[out + k] += TAPS[k + 4]
    return weights.astype(np.float32)


def row_pass_weights():
    weights = np.zeros((8, 256, 128), np.float32)
    for r in range(8):
        for c in range(128):
            for k in range(-4, 5):
                at = c + k
                if at < 0:
                    weights[r, 128 + r * 4 + at + 4, c] = TAPS[k + 4]
                elif at >= 128:
                    weights[r, 160 + r * 4 + at - 128, c] = TAPS[k + 4]
                else:
                    weights[r, at, c] = TAPS[k + 4]
    return weights


def split_rows(x_ref, wr_ref, wc_ref, top_ref, bot_ref, ws_ref):
    acc = jnp.zeros((128, 128), f32)
    for r in range(8):
        row = x_ref[pl.ds(r, 128, stride=8), :]
        if r < 4:
            top_ref[r] = row
        else:
            bot_ref[r - 4] = row
        acc = acc + row * wr_ref[r]
    acc = acc * wc_ref[...]
    ones = jnp.ones((8, 128), f32)
    ws_ref[...] = lax.dot_general(ones, acc, NT, precision=HI, preferred_element_type=f32)[0:1]


def column_pass(above_ref, top_ref, bot_ref, below_ref, v_ref, left_ref, right_ref):
    lane = lax.broadcasted_iota(jnp.int32, (8, 128), 1)

    def step(s, carry):
        at = pl.ds(pl.multiple_of(s * 8, 8), 8)
        left = jnp.zeros((8, 128), f32)
        right = jnp.zeros((8, 128), f32)
        for g in range(4):
            rows = [ref[i, g, at, :] for ref in (above_ref, top_ref, bot_ref, below_ref) for i in range(4)]
            for r in range(8):
                v = rows[r + 4] * TAPS[4]
                for k in range(1, 5):
                    v = v + (rows[r + 4 - k] + rows[r + 4 + k]) * TAPS[4 + k]
                v_ref[r, g, at, :] = v
                slot = g * 32 + r * 4
                here = (lane >= slot) & (lane < slot + 4)
                left = jnp.where(here, pltpu.roll(v, slot, 1) if slot else v, left)
                right = jnp.where(here, pltpu.roll(v, (slot + 4) % 128, 1), right)
        left_ref[at, :] = left
        right_ref[at, :] = right
        return carry

    lax.fori_loop(0, 8, step, 0)


def row_pass(v_ref, left_ref, right_ref, mean_ref, w_ref, u_ref, spread_ref):
    g = pl.program_id(0)
    lane = lax.broadcasted_iota(jnp.int32, (256, 128), 1)
    left = jnp.zeros((256, 128), f32)
    right = jnp.zeros((256, 128), f32)
    for i in range(4):
        here = g == i
        a, b = left_ref[...], right_ref[...]
        left = jnp.where(here, pltpu.roll(a, (128 - 32 * i) % 128, 1) if i else a, left)
        right = jnp.where(here, pltpu.roll(b, (160 - 32 * i) % 128, 1), right)
    halo = jnp.where(lane < 32, left, jnp.where(lane < 64, right, 0.0))
    mean = mean_ref[...]
    acc = jnp.zeros((256, 128), f32)
    for r in range(8):
        wide = jnp.concatenate([v_ref[r], halo], axis=1)
        smooth = jnp.dot(wide, w_ref[r], precision=HI, preferred_element_type=f32)
        centered = smooth - mean
        acc = acc + centered * centered
        u_ref[:, r * 128:(r + 1) * 128] = centered.astype(jnp.bfloat16)
    ones = jnp.ones((8, 128), f32)
    spread_ref[...] = lax.dot_general(ones, acc, NT, precision=HI, preferred_element_type=f32)[0:1]


def gram(core_ref, rows_ref, u_ref, spread_ref, keep_ref, send_ref):
    first = core_ref[0] == 0
    part = lax.dot_general(rows_ref[...], u_ref[...], NT, preferred_element_type=f32)
    sub = lax.broadcasted_iota(jnp.int32, (8, 128), 0)
    for zl in range(4):
        for y in range(4):
            at = (zl * 4 + y) * 16
            for cb in range(8):
                a = part[at:at + 8, cb * 128:(cb + 1) * 128]
                b = part[at + 8:at + 16, cb * 128:(cb + 1) * 128]
                c0 = jnp.where(sub < 4, a, pltpu.roll(b, 4, 0))
                c1 = jnp.where(sub < 4, pltpu.roll(a, 4, 0), b)
                keep_ref[y, zl * 8 + cb] = jnp.where(first, c0, c1)
                send_ref[y, zl * 8 + cb] = jnp.where(first, c1, c0)
    for y in range(4):
        keep_ref[y, 32] = spread_ref[...]
        send_ref[y, 32] = spread_ref[...]


def fold(part_ref, out_ref):
    sub = lax.broadcasted_iota(jnp.int32, (8, 128), 0)
    total = []
    for t in range(33):
        s = part_ref[0, t]
        for p in range(1, 16):
            s = s + part_ref[p, t]
        total.append(s)
    for zl in range(4):
        for k in range(4):
            a, b = total[zl * 8 + 2 * k], total[zl * 8 + 2 * k + 1]
            out_ref[zl * 2, k] = jnp.where(sub < 4, a, pltpu.roll(b, 4, 0))
            out_ref[zl * 2 + 1, k] = jnp.where(sub < 4, pltpu.roll(a, 4, 0), b)
        out_ref[zl * 2, 4] = total[32]
        out_ref[zl * 2 + 1, 4] = total[32]


def finish(place_ref, part_ref, out_ref):
    first_row = place_ref[0] * 4
    total = []
    for t in range(5):
        s = part_ref[0, t]
        for p in range(1, 8):
            s = s + part_ref[p, t]
        total.append(s)
    scale = 1.0 / jnp.sqrt(total[4] + 1e-06)
    sub = lax.broadcasted_iota(jnp.int32, (8, 128), 0)
    lane = lax.broadcasted_iota(jnp.int32, (8, 128), 1)
    flat = sub * 128 + lane
    own = jnp.zeros((8, 128), f32)
    for i in range(4):
        value = jnp.sum(jnp.where(flat == first_row + i, scale, 0.0))
        own = jnp.where((sub & 3) == i, value, own)
    for k in range(4):
        cols = jnp.where(sub < 4, scale[2 * k:2 * k + 1, :], scale[2 * k + 1:2 * k + 2, :])
        tile = total[k] * cols * own
        out_ref[:, 2 * k * 128:(2 * k + 1) * 128] = tile[0:4]
        out_ref[:, (2 * k + 1) * 128:(2 * k + 2) * 128] = tile[4:8]


def local(images):
    shape = jax.ShapeDtypeStruct
    smem = pl.BlockSpec(memory_space=pltpu.SMEM)
    params = pltpu.CompilerParams(vmem_limit_bytes=48 * 1024 * 1024)
    gx_axes, gy_axes = ("x", "zl"), ("y", "zh", "c")
    gx, gy = lax.axis_index(gx_axes), lax.axis_index(gy_axes)

    weight_rows = lax.dynamic_slice(jnp.asarray(edge_weights(128)), (gx * 8,), (8,))
    weight_cols = lax.dynamic_slice(jnp.asarray(edge_weights(2048)), (gy * 128,), (128,)).reshape(1, 128)
    top, bot, weighted = pl.pallas_call(
        split_rows,
        grid=(8,),
        in_specs=[pl.BlockSpec((1024, 128), lambda i: (i, 0)), smem, pl.BlockSpec((1, 128), lambda i: (0, 0))],
        out_specs=[
            pl.BlockSpec((4, 128, 128), lambda i: (0, i, 0)),
            pl.BlockSpec((4, 128, 128), lambda i: (0, i, 0)),
            pl.BlockSpec((1, 128), lambda i: (0, i)),
        ],
        out_shape=[shape((4, 1024, 128), f32), shape((4, 1024, 128), f32), shape((1, 1024), f32)],
        compiler_params=params,
    )(images.reshape(8192, 128), weight_rows, weight_cols)

    up = [(i, i + 1) for i in range(15)]
    down = [(j, i) for i, j in up]
    above = lax.ppermute(bot, gx_axes, up)
    below = lax.ppermute(top, gx_axes, down)
    total = lax.psum(weighted, gx_axes + gy_axes)
    mean = jnp.broadcast_to((total / f32(PIXELS)).reshape(1024, 1), (1024, 128))

    spec = pl.BlockSpec((4, 4, 64, 128), lambda i: (0, 0, i, 0))
    strip = pl.BlockSpec((64, 128), lambda i: (i, 0))
    grouped = [a.reshape(4, 4, 256, 128) for a in (above, top, bot, below)]
    vertical, left, right = pl.pallas_call(
        column_pass,
        grid=(4,),
        in_specs=[spec] * 4,
        out_specs=[pl.BlockSpec((8, 4, 64, 128), lambda i: (0, 0, i, 0)), strip, strip],
        out_shape=[shape((8, 4, 256, 128), f32), shape((256, 128), f32), shape((256, 128), f32)],
        compiler_params=params,
    )(*grouped)
    from_left = lax.ppermute(right, gy_axes, up)
    from_right = lax.ppermute(left, gy_axes, down)

    whole = pl.BlockSpec((256, 128), lambda i: (0, 0))
    unit, spread = pl.pallas_call(
        row_pass,
        grid=(4,),
        in_specs=[
            pl.BlockSpec((8, 256, 128), lambda i: (0, i, 0)),
            whole,
            whole,
            pl.BlockSpec((256, 128), lambda i: (i, 0)),
            pl.BlockSpec((8, 256, 128), lambda i: (0, 0, 0)),
        ],
        out_specs=[pl.BlockSpec((256, 1024), lambda i: (i, 0)), pl.BlockSpec((1, 256), lambda i: (0, i))],
        out_shape=[shape((1024, 1024), jnp.bfloat16), shape((1, 1024), f32)],
        compiler_params=params,
    )(vertical.reshape(8, 1024, 128), from_left, from_right, mean, jnp.asarray(row_pass_weights()))

    core = lax.axis_index("c")
    block = pl.BlockSpec((4, 33, 8, 128), lambda i: (i, 0, 0, 0))
    keep, send = pl.pallas_call(
        gram,
        grid=(4,),
        in_specs=[
            smem,
            pl.BlockSpec((256, 1024), lambda i: (i, 0)),
            pl.BlockSpec((1024, 1024), lambda i: (0, 0)),
            pl.BlockSpec((8, 128), lambda i: (0, 0)),
        ],
        out_specs=[block, block],
        out_shape=[shape((16, 33, 8, 128), f32)] * 2,
        compiler_params=params,
    )(core.reshape(1), unit, unit, spread.reshape(8, 128))

    part = keep + lax.ppermute(send, "c", [(0, 1), (1, 0)])
    part = lax.all_to_all(part, ("x", "y"), 0, 0, tiled=True)
    part = pl.pallas_call(
        fold,
        out_shape=shape((8, 5, 8, 128), f32),
        compiler_params=params,
    )(part)
    part = lax.all_to_all(part, ("zl", "zh"), 0, 0, tiled=True)
    return pl.pallas_call(
        finish,
        in_specs=[smem, pl.BlockSpec(memory_space=pltpu.VMEM)],
        out_shape=shape((4, 1024), f32),
        compiler_params=params,
    )((gx * 16 + gy).reshape(1), part)


def solution(mesh):
    fine = Mesh(mesh.devices.reshape(4, 4, 4, 2, 2), ("x", "zl", "y", "zh", "c"))
    return jax.shard_map(
        local,
        mesh=fine,
        in_specs=(P(None, ("x", "zl"), ("y", "zh", "c")),),
        out_specs=P(("x", "zl", "y", "zh", "c"), None),
        check_vma=False,
    )
```

```python
import functools
import math

import jax
import jax.numpy as jnp
import numpy as np
from jax import lax
from jax.experimental import pallas as pl
from jax.experimental.pallas import tpu as pltpu
from jax.sharding import Mesh, PartitionSpec as P

f32 = jnp.float32
HI = lax.Precision.HIGHEST
NT = (((1,), (1,)), ((), ()))
PIXELS = 128 * 2048
GX, GY = ("x", "zl"), ("y", "zh", "c")
AXES = GX + GY


def stencil_taps():
    raw = [math.exp(-k * k / 4.5) for k in range(-4, 5)]
    total = sum(raw)
    return [value / total for value in raw]


TAPS = stencil_taps()


def edge_weights(length):
    weights = np.zeros(length, np.float64)
    for k in range(-4, 5):
        for out in range(length):
            if 0 <= out + k < length:
                weights[out + k] += TAPS[k + 4]
    return weights.astype(np.float32)


def row_pass_weights():
    weights = np.zeros((8, 256, 128), np.float32)
    for r in range(8):
        for c in range(128):
            for k in range(-4, 5):
                at = c + k
                if at < 0:
                    weights[r, 128 + r * 4 + at + 4, c] = TAPS[k + 4]
                elif at >= 128:
                    weights[r, 160 + r * 4 + at - 128, c] = TAPS[k + 4]
                else:
                    weights[r, at, c] = TAPS[k + 4]
    return weights


def survey(x_ref, wr_ref, wc_ref, left_ref, right_ref, sum_ref):
    gx = lax.axis_index("x") * 4 + lax.axis_index("zl")
    gy = lax.axis_index("y") * 4 + lax.axis_index("zh") * 2 + lax.axis_index("c")
    lane = lax.broadcasted_iota(jnp.int32, (128, 128), 1)
    left = jnp.zeros((128, 128), f32)
    right = jnp.zeros((128, 128), f32)
    cols = wc_ref[pl.ds(gy, 1), :]
    ones = jnp.ones((8, 128), f32)
    for g in range(4):
        acc = jnp.zeros((128, 128), f32)
        for r in range(8):
            row = x_ref[g, pl.ds(r, 128, stride=8), :]
            acc = acc + row * wr_ref[gx * 8 + r]
            slot = g * 32 + r * 4
            here = (lane >= slot) & (lane < slot + 4)
            left = jnp.where(here, pltpu.roll(row, slot, 1) if slot else row, left)
            right = jnp.where(here, pltpu.roll(row, (slot + 4) % 128, 1), right)
        sums = lax.dot_general(ones, acc * cols, NT, precision=HI, preferred_element_type=f32)
        sum_ref[g:g + 1, :] = sums[0:1]
    left_ref[...] = left
    right_ref[...] = right


def row_pass(g, x_ref, left_ref, right_ref, w_ref, order_ref, top_ref, bot_ref):
    lane = lax.broadcasted_iota(jnp.int32, (128, 128), 1)
    left = pltpu.roll(left_ref[...], 128 - 32 * g, 1) if g else left_ref[...]
    right = pltpu.roll(right_ref[...], (160 - 32 * g) % 128, 1) if g != 1 else right_ref[...]
    halo = jnp.where(lane < 32, left, jnp.where(lane < 64, right, 0.0))
    for r in range(8):
        wide = jnp.concatenate([x_ref[0, pl.ds(r, 128, stride=8), :], halo], axis=1)
        smooth = jnp.dot(wide, w_ref[r], precision=HI, preferred_element_type=f32)
        if r < 4:
            top_ref[r] = smooth
        else:
            bot_ref[r - 4] = smooth


def column_pass(q, *refs):
    refs = list(refs)
    above = [refs.pop(0)]
    below = [refs.pop(0)]
    if q < 3:
        above.append(refs.pop(0))
        below.append(refs.pop(0))
    top_ref, bot_ref, mean_ref, u_ref, spread_ref, acc_ref = refs
    x, zl = lax.axis_index("x"), lax.axis_index("zl")
    above_far = (zl == 0) & (x <= 3 - q)
    below_far = (zl == 3) & (x >= q)

    def outer(pair, far, i, at):
        near = pair[0][i, at, :]
        return jnp.where(far, pair[1][i, at, :], near) if len(pair) > 1 else near

    def step(s, carry):
        at = pl.ds(pl.multiple_of(s * 16, 16), 16)
        rows = [outer(above, above_far, i, at) for i in range(4)]
        rows += [ref[i, at, :] for ref in (top_ref, bot_ref) for i in range(4)]
        rows += [outer(below, below_far, i, at) for i in range(4)]
        mean = mean_ref[at, :]
        acc = jnp.zeros((16, 128), f32)
        for r in range(8):
            v = rows[r + 4] * TAPS[4]
            for k in range(1, 5):
                v = v + (rows[r + 4 - k] + rows[r + 4 + k]) * TAPS[4 + k]
            centered = v - mean
            acc = acc + centered * centered
            u_ref[at, r * 128:(r + 1) * 128] = centered.astype(jnp.bfloat16)
        acc_ref[at, :] = acc
        return carry

    lax.fori_loop(0, 8, step, 0)
    ones = jnp.ones((8, 128), f32)
    spread_ref[...] = lax.dot_general(ones, acc_ref[...], NT, precision=HI, preferred_element_type=f32)[0:1]


def gram(u0_ref, u1_ref, u2_ref, u3_ref, spread_ref, keep_ref, send_ref):
    first = lax.axis_index("c") == 0
    units = (u0_ref, u1_ref, u2_ref, u3_ref)
    x = pl.program_id(0)
    rows = u0_ref[...]
    for i in range(1, 4):
        rows = jnp.where(x == i, units[i][...], rows)
    part = jnp.concatenate(
        [lax.dot_general(rows, u[...], NT, preferred_element_type=f32) for u in units], axis=1
    )
    sub = lax.broadcasted_iota(jnp.int32, (8, 128), 0)
    for zl in range(4):
        for y in range(4):
            at = (zl * 4 + y) * 16
            for cb in range(8):
                a = part[at:at + 8, cb * 128:(cb + 1) * 128]
                b = part[at + 8:at + 16, cb * 128:(cb + 1) * 128]
                c0 = jnp.where(sub < 4, a, pltpu.roll(b, 4, 0))
                c1 = jnp.where(sub < 4, pltpu.roll(a, 4, 0), b)
                keep_ref[y, zl * 8 + cb] = jnp.where(first, c0, c1)
                send_ref[y, zl * 8 + cb] = jnp.where(first, c1, c0)
    for y in range(4):
        keep_ref[y, 32] = spread_ref[...]
        send_ref[y, 32] = spread_ref[...]


def fold(part_ref, out_ref):
    sub = lax.broadcasted_iota(jnp.int32, (8, 128), 0)
    total = []
    for t in range(33):
        s = part_ref[0, t]
        for p in range(1, 16):
            s = s + part_ref[p, t]
        total.append(s)
    for zl in range(4):
        for k in range(4):
            a, b = total[zl * 8 + 2 * k], total[zl * 8 + 2 * k + 1]
            out_ref[zl * 2, k] = jnp.where(sub < 4, a, pltpu.roll(b, 4, 0))
            out_ref[zl * 2 + 1, k] = jnp.where(sub < 4, pltpu.roll(a, 4, 0), b)
        out_ref[zl * 2, 4] = total[32]
        out_ref[zl * 2 + 1, 4] = total[32]


def finish(part_ref, out_ref):
    first_row = lax.axis_index(AXES) * 4
    total = []
    for t in range(5):
        s = part_ref[0, t]
        for p in range(1, 8):
            s = s + part_ref[p, t]
        total.append(s)
    scale = 1.0 / jnp.sqrt(total[4] + 1e-06)
    sub = lax.broadcasted_iota(jnp.int32, (8, 128), 0)
    lane = lax.broadcasted_iota(jnp.int32, (8, 128), 1)
    flat = sub * 128 + lane
    own = jnp.zeros((8, 128), f32)
    for i in range(4):
        value = jnp.sum(jnp.where(flat == first_row + i, scale, 0.0))
        own = jnp.where((sub & 3) == i, value, own)
    for k in range(4):
        cols = jnp.where(sub < 4, scale[2 * k:2 * k + 1, :], scale[2 * k + 1:2 * k + 2, :])
        tile = total[k] * cols * own
        out_ref[:, 2 * k * 128:(2 * k + 1) * 128] = tile[0:4]
        out_ref[:, (2 * k + 1) * 128:(2 * k + 2) * 128] = tile[4:8]


def far_pairs(q, upward):
    return [x for x in range(3) if (x < 3 - q if upward else x >= q)]


def exchange(q, top, bot):
    ahead, back = far_pairs(q, True), far_pairs(q, False)
    up = [(i, i + 1) for i in range(15) if not (i % 4 == 3 and i // 4 in ahead)]
    up += [(x * 4 + 3, x * 4) for x in ahead]
    down = [(i + 1, i) for i in range(15) if not (i % 4 == 3 and i // 4 in back)]
    down += [(x * 4 + 4, x * 4 + 7) for x in back]
    above = lax.ppermute(bot, GX, up)
    below = lax.ppermute(top, GX, down)
    if not ahead:
        return above, below
    above_far = lax.ppermute(above, GX, [(x * 4, x * 4 + 4) for x in ahead])
    below_far = lax.ppermute(below, GX, [(x * 4 + 7, x * 4 + 3) for x in back])
    return above, below, above_far, below_far


def all_sum(value, stages):
    for axis, size, bit in stages:
        value = value + lax.ppermute(value, axis, [(i, i ^ bit) for i in range(size)])
    return value


def local(images):
    shape = jax.ShapeDtypeStruct
    vmem = pl.BlockSpec(memory_space=pltpu.VMEM)
    params = pltpu.CompilerParams(vmem_limit_bytes=48 * 1024 * 1024)
    grouped = images.reshape(4, 2048, 128)

    left, right, sums = pl.pallas_call(
        survey,
        grid=(2,),
        in_specs=[
            pl.BlockSpec((4, 1024, 128), lambda i: (0, i, 0)),
            pl.BlockSpec(memory_space=pltpu.SMEM),
            pl.BlockSpec((16, 128), lambda i: (0, 0)),
        ],
        out_specs=[
            pl.BlockSpec((128, 128), lambda i: (i, 0)),
            pl.BlockSpec((128, 128), lambda i: (i, 0)),
            pl.BlockSpec((4, 128), lambda i: (0, i)),
        ],
        out_shape=[shape((256, 128), f32), shape((256, 128), f32), shape((4, 256), f32)],
        compiler_params=params,
    )(grouped, jnp.asarray(edge_weights(128)), jnp.asarray(edge_weights(2048).reshape(16, 128)))

    up = [(i, i + 1) for i in range(15)]
    down = [(j, i) for i, j in up]
    from_left = lax.ppermute(right, GY, up)
    from_right = lax.ppermute(left, GY, down)
    early = all_sum(sums, [("zl", 4, 1), ("zl", 4, 2), ("zh", 2, 1), ("x", 4, 1), ("x", 4, 2)])

    weights = jnp.asarray(row_pass_weights())
    strip = pl.BlockSpec((128, 128), lambda i: (i, 0))
    rows = pl.BlockSpec((4, 128, 128), lambda i: (0, i, 0))
    halves, ghosts = [], []
    for q in range(4):
        top, bot = pl.pallas_call(
            functools.partial(row_pass, q),
            grid=(2,),
            in_specs=[
                pl.BlockSpec((1, 1024, 128), lambda i, q=q: (q, i, 0)),
                strip,
                strip,
                pl.BlockSpec((8, 256, 128), lambda i: (0, 0, 0)),
                pl.BlockSpec(memory_space=pl.ANY),
            ],
            out_specs=[rows, rows],
            out_shape=[shape((4, 256, 128), f32)] * 2,
            compiler_params=params,
        )(grouped, from_left, from_right, weights, halves[-1][0] if q else early)
        halves.append((top, bot))
        ghosts.append(exchange(q, top, bot))

    total = all_sum(early, [("y", 4, 1), ("y", 4, 2), ("c", 2, 1)])
    mean = jnp.broadcast_to((total / f32(PIXELS)).reshape(1024, 1), (1024, 128))

    units, spreads = [], []
    for q in range(4):
        ins = list(ghosts[q]) + list(halves[q])
        unit, spread = pl.pallas_call(
            functools.partial(column_pass, q),
            grid=(2,),
            in_specs=[rows] * len(ins) + [pl.BlockSpec((128, 128), lambda i, q=q: (2 * q + i, 0))],
            out_specs=[pl.BlockSpec((128, 1024), lambda i: (i, 0)), pl.BlockSpec((1, 128), lambda i: (0, i))],
            out_shape=[shape((256, 1024), jnp.bfloat16), shape((1, 256), f32)],
            scratch_shapes=[pltpu.VMEM((128, 128), f32)],
            compiler_params=params,
        )(*ins, mean)
        units.append(unit)
        spreads.append(spread)

    block = pl.BlockSpec((4, 33, 8, 128), lambda i: (i, 0, 0, 0))
    keep, send = pl.pallas_call(
        gram,
        grid=(4,),
        in_specs=[pl.BlockSpec((256, 1024), lambda i: (0, 0))] * 4 + [pl.BlockSpec((8, 128), lambda i: (0, 0))],
        out_specs=[block, block],
        out_shape=[shape((16, 33, 8, 128), f32)] * 2,
        compiler_params=params,
    )(*units, jnp.concatenate(spreads, axis=1).reshape(8, 128))

    part = keep + lax.ppermute(send, "c", [(0, 1), (1, 0)])
    part = lax.all_to_all(part, ("x", "y"), 0, 0, tiled=True)
    part = pl.pallas_call(
        fold,
        in_specs=[vmem],
        out_specs=vmem,
        out_shape=shape((8, 5, 8, 128), f32),
        compiler_params=params,
    )(part)
    part = lax.all_to_all(part, ("zl", "zh"), 0, 0, tiled=True)
    return pl.pallas_call(
        finish,
        in_specs=[vmem],
        out_specs=vmem,
        out_shape=shape((4, 1024), f32),
        compiler_params=params,
    )(part)


def solution(mesh):
    fine = Mesh(mesh.devices.reshape(4, 4, 4, 2, 2), AXES)
    return jax.shard_map(
        local,
        mesh=fine,
        in_specs=(P(None, GX, GY),),
        out_specs=P(AXES, None),
        check_vma=False,
    )
```

```python
import functools
import math

import jax
import jax.numpy as jnp
from jax import lax
from jax.experimental import pallas as pl
from jax.experimental.pallas import tpu as pltpu
from jax.sharding import Mesh, PartitionSpec as P

f32 = jnp.float32
HI = lax.Precision.HIGHEST
NT = (((1,), (1,)), ((), ()))
TILE = 8 * 128
GX, GY = ("x", "zl"), ("y", "zh", "c")
AXES = GX + GY


def stencil_taps():
    raw = [math.exp(-k * k / 4.5) for k in range(-4, 5)]
    total = sum(raw)
    return [value / total for value in raw]


TAPS = stencil_taps()


def survey(x_ref, left_ref, right_ref):
    lane = lax.broadcasted_iota(jnp.int32, (64, 128), 1)
    left = jnp.zeros((64, 128), f32)
    right = jnp.zeros((64, 128), f32)
    for g in range(4):
        for r in range(8):
            row = x_ref[g, pl.ds(r, 64, stride=8), :]
            slot = g * 32 + r * 4
            here = (lane >= slot) & (lane < slot + 4)
            left = jnp.where(here, pltpu.roll(row, slot, 1) if slot else row, left)
            right = jnp.where(here, pltpu.roll(row, (slot + 4) % 128, 1), right)
    left_ref[...] = left
    right_ref[...] = right


def row_pass(first_group, x_ref, left_ref, right_ref, order_ref, top_ref, bot_ref):
    turn = 128 - 32 * (first_group + pl.program_id(0))
    lane = lax.broadcasted_iota(jnp.int32, (8, 128), 1)

    def step(s, carry):
        at = pl.ds(pl.multiple_of(s * 8, 8), 8)
        left = pltpu.roll(left_ref[at, :], turn, 1)
        right = pltpu.roll(right_ref[at, :], turn, 1)
        for r in range(8):
            row = x_ref[0, pl.ds(s * 64 + r, 8, stride=8), :]
            ends = jnp.where(
                lane < 64,
                pltpu.roll(right, 128 - 4 * r, 1) if r else right,
                pltpu.roll(left, 124 - 4 * r, 1),
            )
            smooth = row * TAPS[4]
            for k in range(1, 5):
                after = pltpu.roll(jnp.where(lane < k, ends, row), 128 - k, 1)
                before = pltpu.roll(jnp.where(lane >= 128 - k, ends, row), k, 1)
                smooth = smooth + (after + before) * TAPS[4 + k]
            if r < 4:
                top_ref[r, at, :] = smooth
            else:
                bot_ref[r - 4, at, :] = smooth
        return carry

    lax.fori_loop(0, 16, step, 0)


def column_pass(above_ref, below_ref, top_ref, bot_ref, u_ref, spread_ref, mean_ref, square_ref, level_ref):
    def step(s, carry):
        at = pl.ds(pl.multiple_of(s * 16, 16), 16)
        rows = [ref[i, at, :] for ref in (above_ref, top_ref, bot_ref, below_ref) for i in range(4)]
        smooth = []
        for r in range(8):
            v = rows[r + 4] * TAPS[4]
            for k in range(1, 5):
                v = v + (rows[r + 4 - k] + rows[r + 4 + k]) * TAPS[4 + k]
            smooth.append(v)
        total = ((smooth[0] + smooth[1]) + (smooth[2] + smooth[3])) + ((smooth[4] + smooth[5]) + (smooth[6] + smooth[7]))
        mean = jnp.sum(total, axis=1, keepdims=True) * f32(1.0 / TILE)
        acc = jnp.zeros((16, 128), f32)
        for r in range(8):
            centered = smooth[r] - mean
            acc = acc + centered * centered
            u_ref[at, r * 128:(r + 1) * 128] = centered.astype(jnp.bfloat16)
        square_ref[at, :] = acc
        level_ref[at, :] = jnp.broadcast_to(mean, (16, 128))
        return carry

    lax.fori_loop(0, 8, step, 0)
    ones = jnp.ones((8, 128), f32)
    pick = jnp.where(lax.broadcasted_iota(jnp.int32, (8, 128), 1) == 0, f32(1), f32(0))
    spread_ref[...] = lax.dot_general(ones, square_ref[...], NT, precision=HI, preferred_element_type=f32)[0:1]
    mean_ref[...] = lax.dot_general(pick, level_ref[...], NT, precision=HI, preferred_element_type=f32)[0:1]


def gram(u0_ref, u1_ref, spread_ref, mean_ref, keep_ref, send_ref):
    first = lax.axis_index("c") == 0
    x = pl.program_id(0)
    at = pl.ds(pl.multiple_of((x % 2) * 256, 256), 256)
    rows = jnp.where(x < 2, u0_ref[at, :], u1_ref[at, :])
    part = jnp.concatenate(
        [lax.dot_general(rows, u[...], NT, preferred_element_type=f32) for u in (u0_ref, u1_ref)], axis=1
    )
    sub = lax.broadcasted_iota(jnp.int32, (8, 128), 0)
    for zl in range(4):
        for y in range(4):
            at = (zl * 4 + y) * 16
            for cb in range(8):
                a = part[at:at + 8, cb * 128:(cb + 1) * 128]
                b = part[at + 8:at + 16, cb * 128:(cb + 1) * 128]
                c0 = jnp.where(sub < 4, a, pltpu.roll(b, 4, 0))
                c1 = jnp.where(sub < 4, pltpu.roll(a, 4, 0), b)
                keep_ref[y, zl * 8 + cb] = jnp.where(first, c0, c1)
                send_ref[y, zl * 8 + cb] = jnp.where(first, c1, c0)
    for y in range(4):
        for ref, own, other in ((keep_ref, 33, 34), (send_ref, 34, 33)):
            ref[y, 32] = spread_ref[...]
            ref[y, own] = mean_ref[...]
            ref[y, other] = jnp.zeros((8, 128), f32)


def between(shift_ref, select):
    wide = jnp.concatenate([shift_ref[cb] for cb in range(8)], axis=1)
    rows = [
        lax.dot_general(one_hot, shift_ref[block], NT, precision=HI, preferred_element_type=f32)
        for block, one_hot in select
    ]
    rows = jnp.concatenate(rows, axis=0) if len(rows) > 1 else rows[0]
    return jnp.dot(rows, wide, precision=HI, preferred_element_type=f32)


def fold(part_ref, out_ref, shift_ref):
    x, y, c = lax.axis_index("x"), lax.axis_index("y"), lax.axis_index("c")
    sub = lax.broadcasted_iota(jnp.int32, (8, 128), 0)
    lane = lax.broadcasted_iota(jnp.int32, (8, 128), 1)

    def summed(t):
        s = part_ref[0, t]
        for p in range(1, 16):
            s = s + part_ref[p, t]
        return s

    mean = (summed(33) + summed(34)) * f32(1.0 / 32)
    spread = summed(32)
    for k in range(2):
        for p in range(16):
            shift = part_ref[p, 33 + k] - mean
            spread = spread + shift * shift * f32(TILE)
            for cb in range(8):
                shift_ref[cb, k * 16 + p:k * 16 + p + 1, :] = shift[cb:cb + 1]
    select = []
    for zl in range(4):
        want = (zl % 2) * 64 + y * 16 + (sub // 4) * 8 + c * 4 + sub % 4
        select.append((2 * x + zl // 2, jnp.where(lane == want, f32(1), f32(0))))
    extra = between(shift_ref, select) * f32(TILE)
    for zl in range(4):
        for k in range(4):
            a, b = [
                summed(zl * 8 + cb) + extra[zl * 8:zl * 8 + 8, cb * 128:(cb + 1) * 128] for cb in (2 * k, 2 * k + 1)
            ]
            out_ref[zl * 2, k] = jnp.where(sub < 4, a, pltpu.roll(b, 4, 0))
            out_ref[zl * 2 + 1, k] = jnp.where(sub < 4, pltpu.roll(a, 4, 0), b)
        for zh in range(2):
            out_ref[zl * 2 + zh, 4] = spread
            out_ref[zl * 2 + zh, 5] = mean


def finish(part_ref, out_ref, shift_ref):
    first_row = lax.axis_index(AXES) * 4
    sub = lax.broadcasted_iota(jnp.int32, (8, 128), 0)
    lane = lax.broadcasted_iota(jnp.int32, (8, 128), 1)

    def summed(t):
        s = part_ref[0, t]
        for p in range(1, 8):
            s = s + part_ref[p, t]
        return s

    mean = summed(5) * f32(1.0 / 8)
    spread = summed(4)
    for p in range(8):
        shift = part_ref[p, 5] - mean
        spread = spread + shift * shift * f32(32 * TILE)
        for cb in range(8):
            shift_ref[cb, p:p + 1, :] = shift[cb:cb + 1]
    one_hot = jnp.where(lane == first_row % 128 + sub % 4, f32(1), f32(0))
    extra = between(shift_ref, [(first_row // 128, one_hot)]) * f32(32 * TILE)
    scale = 1.0 / jnp.sqrt(spread + 1e-06)
    flat = sub * 128 + lane
    own = jnp.zeros((8, 128), f32)
    for i in range(4):
        value = jnp.sum(jnp.where(flat == first_row + i, scale, 0.0))
        own = jnp.where((sub & 3) == i, value, own)
    for k in range(4):
        at, to = 2 * k * 128, (2 * k + 1) * 128
        cols = jnp.where(sub < 4, scale[2 * k:2 * k + 1, :], scale[2 * k + 1:2 * k + 2, :])
        more = jnp.where(sub < 4, extra[:, at:to], extra[:, to:to + 128])
        tile = (summed(k) + more) * cols * own
        out_ref[:, at:to] = tile[0:4]
        out_ref[:, to:to + 128] = tile[4:8]


def local(images):
    shape = jax.ShapeDtypeStruct
    vmem = pl.BlockSpec(memory_space=pltpu.VMEM)
    params = pltpu.CompilerParams(vmem_limit_bytes=48 * 1024 * 1024)
    grouped = images.reshape(4, 2048, 128)
    up = [(i, i + 1) for i in range(15)]
    down = [(j, i) for i, j in up]

    strip = pl.BlockSpec((64, 128), lambda i: (i, 0))
    left, right = pl.pallas_call(
        survey,
        grid=(4,),
        in_specs=[pl.BlockSpec((4, 512, 128), lambda i: (0, i, 0))],
        out_specs=[strip, strip],
        out_shape=[shape((256, 128), f32)] * 2,
        compiler_params=params,
    )(grouped)
    from_left = lax.ppermute(right, GY, up)
    from_right = lax.ppermute(left, GY, down)

    halves, ghosts = [], []
    strip = pl.BlockSpec((128, 128), lambda g, i: (i, 0))
    rows = pl.BlockSpec((4, 128, 128), lambda g, i: (0, 2 * g + i, 0))
    for q in range(2):
        top, bot = pl.pallas_call(
            functools.partial(row_pass, 2 * q),
            grid=(2, 2),
            in_specs=[
                pl.BlockSpec((1, 1024, 128), lambda g, i, q=q: (2 * q + g, i, 0)),
                strip,
                strip,
                pl.BlockSpec(memory_space=pl.ANY),
            ],
            out_specs=[rows, rows],
            out_shape=[shape((4, 512, 128), f32)] * 2,
            compiler_params=params,
        )(grouped, from_left, from_right, halves[-1][0] if q else from_left)
        halves.append((top, bot))
        ghosts.append((lax.ppermute(bot, GX, up), lax.ppermute(top, GX, down)))

    units, spreads, means = [], [], []
    rows = pl.BlockSpec((4, 128, 128), lambda i: (0, i, 0))
    line = pl.BlockSpec((1, 128), lambda i: (0, i))
    for q in range(2):
        unit, spread, mean = pl.pallas_call(
            column_pass,
            grid=(4,),
            in_specs=[rows] * 4,
            out_specs=[pl.BlockSpec((128, 1024), lambda i: (i, 0)), line, line],
            out_shape=[shape((512, 1024), jnp.bfloat16), shape((1, 512), f32), shape((1, 512), f32)],
            scratch_shapes=[pltpu.VMEM((128, 128), f32)] * 2,
            compiler_params=params,
        )(*ghosts[q], *halves[q])
        units.append(unit)
        spreads.append(spread)
        means.append(mean)
    spread = jnp.concatenate(spreads, axis=1).reshape(8, 128)
    mean = jnp.concatenate(means, axis=1).reshape(8, 128)

    block = pl.BlockSpec((4, 35, 8, 128), lambda i: (i, 0, 0, 0))
    unit = pl.BlockSpec((512, 1024), lambda i: (0, 0))
    tile = pl.BlockSpec((8, 128), lambda i: (0, 0))
    keep, send = pl.pallas_call(
        gram,
        grid=(4,),
        in_specs=[unit, unit, tile, tile],
        out_specs=[block, block],
        out_shape=[shape((16, 35, 8, 128), f32)] * 2,
        compiler_params=params,
    )(*units, spread, mean)

    part = keep + lax.ppermute(send, "c", [(0, 1), (1, 0)])
    part = lax.all_to_all(part, ("x", "y"), 0, 0, tiled=True)
    part = pl.pallas_call(
        fold,
        in_specs=[vmem],
        out_specs=vmem,
        out_shape=shape((8, 6, 8, 128), f32),
        scratch_shapes=[pltpu.VMEM((8, 32, 128), f32)],
        compiler_params=params,
    )(part)
    part = lax.all_to_all(part, ("zl", "zh"), 0, 0, tiled=True)
    return pl.pallas_call(
        finish,
        in_specs=[vmem],
        out_specs=vmem,
        out_shape=shape((4, 1024), f32),
        scratch_shapes=[pltpu.VMEM((8, 8, 128), f32)],
        compiler_params=params,
    )(part)


def solution(mesh):
    fine = Mesh(mesh.devices.reshape(4, 4, 4, 2, 2), AXES)
    return jax.shard_map(
        local,
        mesh=fine,
        in_specs=(P(None, GX, GY),),
        out_specs=P(AXES, None),
        check_vma=False,
    )
```

```python
import functools
import math

import jax
import jax.numpy as jnp
from jax import lax
from jax.experimental import pallas as pl
from jax.experimental.pallas import tpu as pltpu
from jax.sharding import Mesh, PartitionSpec as P

f32 = jnp.float32
HI = lax.Precision.HIGHEST
NT = (((1,), (1,)), ((), ()))
TILE = 8 * 128
GX, GY = ("x", "zl"), ("y", "zh", "c")
AXES = GX + GY


def stencil_taps():
    raw = [math.exp(-k * k / 4.5) for k in range(-4, 5)]
    total = sum(raw)
    return [value / total for value in raw]


TAPS = stencil_taps()


def survey(x_ref, left_ref, right_ref):
    lane = lax.broadcasted_iota(jnp.int32, (64, 128), 1)
    left = jnp.zeros((64, 128), f32)
    right = jnp.zeros((64, 128), f32)
    for g in range(4):
        for r in range(8):
            row = x_ref[g, pl.ds(r, 64, stride=8), :]
            slot = g * 32 + r * 4
            here = (lane >= slot) & (lane < slot + 4)
            left = jnp.where(here, pltpu.roll(row, slot, 1) if slot else row, left)
            right = jnp.where(here, pltpu.roll(row, (slot + 4) % 128, 1), right)
    left_ref[...] = left
    right_ref[...] = right


def build_weights(order_ref, w_ref):
    at = lax.broadcasted_iota(jnp.int32, (128, 128), 0)
    col = lax.broadcasted_iota(jnp.int32, (128, 128), 1)

    def taps(distance):
        value = jnp.zeros((128, 128), f32)
        for k in range(5):
            value = jnp.where(distance == k, f32(TAPS[4 + k]), value)
        return value

    band = taps(jnp.abs(at - col))
    halo = taps(jnp.abs(at % 4 + jnp.where(at < 32, -4, 128) - col))
    for r in range(8):
        w_ref[r, 0:128] = band
        w_ref[r, 128:256] = jnp.where((at < 64) & (at % 32 // 4 == r), halo, 0.0)


def halo_lanes(g, left, right):
    lane = lax.broadcasted_iota(jnp.int32, left.shape, 1)
    left = pltpu.roll(left, (128 - 32 * g) % 128, 1) if g else left
    right = pltpu.roll(right, (160 - 32 * g) % 128, 1) if g != 1 else right
    return jnp.where(lane < 32, left, jnp.where(lane < 64, right, 0.0))


def smooth_row(row, halo, w):
    wide = jnp.concatenate([row, halo], axis=1)
    return jnp.dot(wide, w, precision=HI, preferred_element_type=f32)


def row_pass(group, count, x_ref, left_ref, right_ref, w_ref, order_ref, top_ref, bot_ref):
    for part in range(2 * count):
        at = slice(part * 128, (part + 1) * 128)
        edge = slice(part % 2 * 128, part % 2 * 128 + 128)
        halo = halo_lanes(group + part // 2, left_ref[edge], right_ref[edge])
        for r in range(8):
            smooth = smooth_row(x_ref[2 * group + part, pl.ds(r, 128, stride=8), :], halo, w_ref[r])
            if r < 4:
                top_ref[r, at] = smooth
            else:
                bot_ref[r - 4, at] = smooth


def to_lanes(squares, level):
    ones = jnp.ones((8, 128), f32)
    pick = jnp.where(lax.broadcasted_iota(jnp.int32, (8, 128), 1) == 0, f32(1), f32(0))
    spread = lax.dot_general(ones, squares, NT, precision=HI, preferred_element_type=f32)
    mean = lax.dot_general(pick, level, NT, precision=HI, preferred_element_type=f32)
    return spread[0:1], mean[0:1]


def smooth_down(rows):
    smooth = []
    for r in range(8):
        v = rows[r + 4] * TAPS[4]
        for k in range(1, 5):
            v = v + (rows[r + 4 - k] + rows[r + 4 + k]) * TAPS[4 + k]
        smooth.append(v)
    return smooth


def column_pass(above_ref, top_ref, bot_ref, below_ref, order_ref, u_ref, spread_ref, mean_ref, square_ref, level_ref):
    def step(s, carry):
        at = pl.ds(pl.multiple_of(s * 16, 16), 16)
        smooth = smooth_down([ref[i, at, :] for ref in (above_ref, top_ref, bot_ref, below_ref) for i in range(4)])
        total = ((smooth[0] + smooth[1]) + (smooth[2] + smooth[3])) + ((smooth[4] + smooth[5]) + (smooth[6] + smooth[7]))
        mean = jnp.sum(total, axis=1, keepdims=True) * f32(1.0 / TILE)
        acc = jnp.zeros((16, 128), f32)
        for r in range(8):
            centered = smooth[r] - mean
            acc = acc + centered * centered
            u_ref[at, r * 128:(r + 1) * 128] = centered.astype(jnp.bfloat16)
        square_ref[at, :] = acc
        level_ref[at, :] = jnp.broadcast_to(mean, (16, 128))
        return carry

    lax.fori_loop(0, square_ref.shape[0] // 16, step, 0, unroll=4)
    spread_ref[...], mean_ref[...] = to_lanes(square_ref[...], level_ref[...])


def gram(u0_ref, u1_ref, u2_ref, spread_ref, mean_ref, keep_ref, send_ref):
    first = lax.axis_index("c") == 0
    units = (u0_ref, u1_ref, u2_ref)
    x = pl.program_id(0)
    rows = jnp.where(x == 0, u0_ref[...], jnp.where(x == 3, u2_ref[...], u1_ref[pl.ds(jnp.where(x == 2, 256, 0), 256), :]))
    part = jnp.concatenate(
        [lax.dot_general(rows, u[...], NT, preferred_element_type=f32) for u in units], axis=1
    )
    sub = lax.broadcasted_iota(jnp.int32, (8, 128), 0)
    for zl in range(4):
        for y in range(4):
            at = (zl * 4 + y) * 16
            for cb in range(8):
                a = part[at:at + 8, cb * 128:(cb + 1) * 128]
                b = part[at + 8:at + 16, cb * 128:(cb + 1) * 128]
                c0 = jnp.where(sub < 4, a, pltpu.roll(b, 4, 0))
                c1 = jnp.where(sub < 4, pltpu.roll(a, 4, 0), b)
                keep_ref[y, zl * 8 + cb] = jnp.where(first, c0, c1)
                send_ref[y, zl * 8 + cb] = jnp.where(first, c1, c0)
    for y in range(4):
        for ref, own, other in ((keep_ref, 33, 34), (send_ref, 34, 33)):
            ref[y, 32] = spread_ref[...]
            ref[y, own] = mean_ref[...]
            ref[y, other] = jnp.zeros((8, 128), f32)


def between(shift_ref, select):
    wide = jnp.concatenate([shift_ref[cb] for cb in range(8)], axis=1)
    rows = [
        lax.dot_general(one_hot, shift_ref[block], NT, precision=HI, preferred_element_type=f32)
        for block, one_hot in select
    ]
    rows = jnp.concatenate(rows, axis=0) if len(rows) > 1 else rows[0]
    return jnp.dot(rows, wide, precision=HI, preferred_element_type=f32)


def fold(part_ref, out_ref, shift_ref):
    x, y, c = lax.axis_index("x"), lax.axis_index("y"), lax.axis_index("c")
    sub = lax.broadcasted_iota(jnp.int32, (8, 128), 0)
    lane = lax.broadcasted_iota(jnp.int32, (8, 128), 1)

    def summed(t):
        s = part_ref[0, t]
        for p in range(1, 16):
            s = s + part_ref[p, t]
        return s

    mean = (summed(33) + summed(34)) * f32(1.0 / 32)
    spread = summed(32)
    for k in range(2):
        for p in range(16):
            shift = part_ref[p, 33 + k] - mean
            spread = spread + shift * shift * f32(TILE)
            for cb in range(8):
                shift_ref[cb, k * 16 + p:k * 16 + p + 1, :] = shift[cb:cb + 1]
    select = []
    for zl in range(4):
        want = (zl % 2) * 64 + y * 16 + (sub // 4) * 8 + c * 4 + sub % 4
        select.append((2 * x + zl // 2, jnp.where(lane == want, f32(1), f32(0))))
    extra = between(shift_ref, select) * f32(TILE)
    for zl in range(4):
        for k in range(4):
            a, b = [
                summed(zl * 8 + cb) + extra[zl * 8:zl * 8 + 8, cb * 128:(cb + 1) * 128] for cb in (2 * k, 2 * k + 1)
            ]
            out_ref[zl * 2, k] = jnp.where(sub < 4, a, pltpu.roll(b, 4, 0))
            out_ref[zl * 2 + 1, k] = jnp.where(sub < 4, pltpu.roll(a, 4, 0), b)
        for zh in range(2):
            out_ref[zl * 2 + zh, 4] = spread
            out_ref[zl * 2 + zh, 5] = mean


def finish(part_ref, out_ref, shift_ref):
    first_row = lax.axis_index(AXES) * 4
    sub = lax.broadcasted_iota(jnp.int32, (8, 128), 0)
    lane = lax.broadcasted_iota(jnp.int32, (8, 128), 1)

    def summed(t):
        s = part_ref[0, t]
        for p in range(1, 8):
            s = s + part_ref[p, t]
        return s

    mean = summed(5) * f32(1.0 / 8)
    spread = summed(4)
    for p in range(8):
        shift = part_ref[p, 5] - mean
        spread = spread + shift * shift * f32(32 * TILE)
        for cb in range(8):
            shift_ref[cb, p:p + 1, :] = shift[cb:cb + 1]
    one_hot = jnp.where(lane == first_row % 128 + sub % 4, f32(1), f32(0))
    extra = between(shift_ref, [(first_row // 128, one_hot)]) * f32(32 * TILE)
    scale = 1.0 / jnp.sqrt(spread + 1e-06)
    flat = sub * 128 + lane
    own = jnp.zeros((8, 128), f32)
    for i in range(4):
        value = jnp.sum(jnp.where(flat == first_row + i, scale, 0.0))
        own = jnp.where((sub & 3) == i, value, own)
    for k in range(4):
        at, to = 2 * k * 128, (2 * k + 1) * 128
        cols = jnp.where(sub < 4, scale[2 * k:2 * k + 1, :], scale[2 * k + 1:2 * k + 2, :])
        more = jnp.where(sub < 4, extra[:, at:to], extra[:, to:to + 128])
        tile = (summed(k) + more) * cols * own
        out_ref[:, at:to] = tile[0:4]
        out_ref[:, to:to + 128] = tile[4:8]


def local(images):
    shape = jax.ShapeDtypeStruct
    vmem = pl.BlockSpec(memory_space=pltpu.VMEM)
    anywhere = pl.BlockSpec(memory_space=pl.ANY)
    params = pltpu.CompilerParams(vmem_limit_bytes=48 * 1024 * 1024)
    by_group = images.reshape(4, 2048, 128)
    by_eighth = images.reshape(8, 1024, 128)
    up = [(i, i + 1) for i in range(15)]
    down = [(j, i) for i, j in up]
    edge_shape = [shape((256, 128), f32)] * 2

    def unit_shape(count):
        return [shape((count, 1024), jnp.bfloat16), shape((1, count), f32), shape((1, count), f32)]

    def swap(axes, ahead, back):
        return lax.ppermute(ahead, axes, up), lax.ppermute(back, axes, down)

    left, right = pl.pallas_call(
        survey,
        grid=(4,),
        in_specs=[pl.BlockSpec((4, 512, 128), lambda i: (0, i, 0))],
        out_specs=[pl.BlockSpec((64, 128), lambda i: (i, 0))] * 2,
        out_shape=edge_shape,
        compiler_params=params,
    )(by_group)
    edges = swap(GY, right, left)
    weights = pl.pallas_call(
        build_weights,
        in_specs=[anywhere],
        out_specs=vmem,
        out_shape=shape((8, 256, 128), f32),
        compiler_params=params,
    )(left)

    def smooth_rows(group, count, order):
        top, bot = pl.pallas_call(
            functools.partial(row_pass, group, count),
            in_specs=[vmem] * 4 + [anywhere],
            out_specs=[vmem] * 2,
            out_shape=[shape((4, 256 * count, 128), f32)] * 2,
            compiler_params=params,
        )(by_eighth, *edges, weights, order)
        above, below = swap(GX, bot, top)
        return above, top, bot, below

    chunks = [smooth_rows(0, 1, left)]
    chunks.append(smooth_rows(1, 2, chunks[0][1]))
    chunks.append(smooth_rows(3, 1, chunks[1][1]))
    results = []
    for count, sources in zip((256, 512, 256), chunks):
        results.append(
            pl.pallas_call(
                column_pass,
                in_specs=[vmem] * 4 + [anywhere],
                out_specs=[vmem] * 3,
                out_shape=unit_shape(count),
                scratch_shapes=[pltpu.VMEM((count, 128), f32)] * 2,
                compiler_params=params,
            )(*sources, results[-1][0] if results else left)
        )
    units, spreads, means = zip(*results)
    spread = jnp.concatenate(spreads, axis=1).reshape(8, 128)
    mean = jnp.concatenate(means, axis=1).reshape(8, 128)

    block = pl.BlockSpec((4, 35, 8, 128), lambda i: (i, 0, 0, 0))
    held = [pl.BlockSpec((n, 1024), lambda i: (0, 0)) for n in (256, 512, 256)]
    tile = pl.BlockSpec((8, 128), lambda i: (0, 0))
    keep, send = pl.pallas_call(
        gram,
        grid=(4,),
        in_specs=held + [tile, tile],
        out_specs=[block, block],
        out_shape=[shape((16, 35, 8, 128), f32)] * 2,
        compiler_params=params,
    )(*units, spread, mean)

    part = keep + lax.ppermute(send, "c", [(0, 1), (1, 0)])
    part = lax.all_to_all(part, ("x", "y"), 0, 0, tiled=True)
    part = pl.pallas_call(
        fold,
        in_specs=[vmem],
        out_specs=vmem,
        out_shape=shape((8, 6, 8, 128), f32),
        scratch_shapes=[pltpu.VMEM((8, 32, 128), f32)],
        compiler_params=params,
    )(part)
    part = lax.all_to_all(part, ("zl", "zh"), 0, 0, tiled=True)
    return pl.pallas_call(
        finish,
        in_specs=[vmem],
        out_specs=vmem,
        out_shape=shape((4, 1024), f32),
        scratch_shapes=[pltpu.VMEM((8, 8, 128), f32)],
        compiler_params=params,
    )(part)


def solution(mesh):
    fine = Mesh(mesh.devices.reshape(4, 4, 4, 2, 2), AXES)
    return jax.shard_map(
        local,
        mesh=fine,
        in_specs=(P(None, GX, GY),),
        out_specs=P(AXES, None),
        check_vma=False,
    )
```

```python
import functools
import math

import jax
import jax.numpy as jnp
from jax import lax
from jax.experimental import pallas as pl
from jax.experimental.pallas import tpu as pltpu
from jax.sharding import Mesh, PartitionSpec as P

f32 = jnp.float32
HI = lax.Precision.HIGHEST
NT = (((1,), (1,)), ((), ()))
TILE = 8 * 128
PARTS = (
    ((0, 0), (0, 1), (1, 0), (1, 1)),
    ((2, 0), (2, 1), (2, 2), (0, 2), (1, 2)),
    ((3, 0), (3, 1), (3, 2), (3, 3), (0, 3), (1, 3), (2, 3)),
)
GX, GY = ("x", "zl"), ("y", "zh", "c")
AXES = GX + GY


def stencil_taps():
    raw = [math.exp(-k * k / 4.5) for k in range(-4, 5)]
    total = sum(raw)
    return [value / total for value in raw]


TAPS = stencil_taps()


def survey(x_ref, left_ref, right_ref):
    lane = lax.broadcasted_iota(jnp.int32, (64, 128), 1)
    left = jnp.zeros((64, 128), f32)
    right = jnp.zeros((64, 128), f32)
    for g in range(4):
        for r in range(8):
            row = x_ref[g, pl.ds(r, 64, stride=8), :]
            slot = g * 32 + r * 4
            here = (lane >= slot) & (lane < slot + 4)
            left = jnp.where(here, pltpu.roll(row, slot, 1) if slot else row, left)
            right = jnp.where(here, pltpu.roll(row, (slot + 4) % 128, 1), right)
    left_ref[...] = left
    right_ref[...] = right


def build_weights(order_ref, w_ref):
    at = lax.broadcasted_iota(jnp.int32, (128, 128), 0)
    col = lax.broadcasted_iota(jnp.int32, (128, 128), 1)

    def taps(distance):
        value = jnp.zeros((128, 128), f32)
        for k in range(5):
            value = jnp.where(distance == k, f32(TAPS[4 + k]), value)
        return value

    band = taps(jnp.abs(at - col))
    halo = taps(jnp.abs(at % 4 + jnp.where(at < 32, -4, 128) - col))
    for r in range(8):
        w_ref[r, 0:128] = band
        w_ref[r, 128:256] = jnp.where((at < 64) & (at % 32 // 4 == r), halo, 0.0)


def halo_lanes(g, left, right):
    lane = lax.broadcasted_iota(jnp.int32, left.shape, 1)
    left = pltpu.roll(left, (128 - 32 * g) % 128, 1) if g else left
    right = pltpu.roll(right, (160 - 32 * g) % 128, 1) if g != 1 else right
    return jnp.where(lane < 32, left, jnp.where(lane < 64, right, 0.0))


def smooth_row(row, halo, w):
    wide = jnp.concatenate([row, halo], axis=1)
    return jnp.dot(wide, w, precision=HI, preferred_element_type=f32)


def row_pass(group, count, x_ref, left_ref, right_ref, w_ref, order_ref, top_ref, bot_ref):
    for part in range(2 * count):
        at = slice(part * 128, (part + 1) * 128)
        edge = slice(part % 2 * 128, part % 2 * 128 + 128)
        halo = halo_lanes(group + part // 2, left_ref[edge], right_ref[edge])
        for r in range(8):
            smooth = smooth_row(x_ref[2 * group + part, pl.ds(r, 128, stride=8), :], halo, w_ref[r])
            if r < 4:
                top_ref[r, at] = smooth
            else:
                bot_ref[r - 4, at] = smooth


def to_lanes(squares, level):
    ones = jnp.ones((8, 128), f32)
    pick = jnp.where(lax.broadcasted_iota(jnp.int32, (8, 128), 1) == 0, f32(1), f32(0))
    spread = lax.dot_general(ones, squares, NT, precision=HI, preferred_element_type=f32)
    mean = lax.dot_general(pick, level, NT, precision=HI, preferred_element_type=f32)
    return spread[0:1], mean[0:1]


def smooth_down(rows):
    smooth = []
    for r in range(8):
        v = rows[r + 4] * TAPS[4]
        for k in range(1, 5):
            v = v + (rows[r + 4 - k] + rows[r + 4 + k]) * TAPS[4 + k]
        smooth.append(v)
    return smooth


def column_pass(above_ref, top_ref, bot_ref, below_ref, *refs):
    u_ref, spread_ref, mean_ref, square_ref, level_ref = refs[-5:]

    def step(s, carry):
        at = pl.ds(pl.multiple_of(s * 16, 16), 16)
        smooth = smooth_down([ref[i, at, :] for ref in (above_ref, top_ref, bot_ref, below_ref) for i in range(4)])
        total = ((smooth[0] + smooth[1]) + (smooth[2] + smooth[3])) + ((smooth[4] + smooth[5]) + (smooth[6] + smooth[7]))
        mean = jnp.sum(total, axis=1, keepdims=True) * f32(1.0 / TILE)
        acc = jnp.zeros((16, 128), f32)
        for r in range(8):
            centered = smooth[r] - mean
            acc = acc + centered * centered
            u_ref[at, r * 128:(r + 1) * 128] = centered.astype(jnp.bfloat16)
        square_ref[at, :] = acc
        level_ref[at, :] = jnp.broadcast_to(mean, (16, 128))
        return carry

    lax.fori_loop(0, square_ref.shape[0] // 16, step, 0, unroll=4)
    spread_ref[...], mean_ref[...] = to_lanes(square_ref[...], level_ref[...])


def gram(blocks, *refs):
    count = 1 + max(a for a, b in blocks)
    units, refs = refs[:count], refs[count:]
    vectors, (keep_ref, send_ref) = refs[:-2], refs[-2:]
    first = lax.axis_index("c") == 0
    sub = lax.broadcasted_iota(jnp.int32, (8, 128), 0)
    for n, (row, col) in enumerate(blocks):
        part = lax.dot_general(units[row][...], units[col][...], NT, preferred_element_type=f32)
        for zl in range(4):
            for y in range(4):
                at = (zl * 4 + y) * 16
                for cb in range(2):
                    a = part[at:at + 8, cb * 128:(cb + 1) * 128]
                    b = part[at + 8:at + 16, cb * 128:(cb + 1) * 128]
                    c0 = jnp.where(sub < 4, a, pltpu.roll(b, 4, 0))
                    c1 = jnp.where(sub < 4, pltpu.roll(a, 4, 0), b)
                    keep_ref[y, n * 8 + zl * 2 + cb] = jnp.where(first, c0, c1)
                    send_ref[y, n * 8 + zl * 2 + cb] = jnp.where(first, c1, c0)
    if vectors:
        spread_ref, mean_ref = vectors
        end = len(blocks) * 8
        for y in range(4):
            for ref, own, other in ((keep_ref, 1, 2), (send_ref, 2, 1)):
                ref[y, end] = spread_ref[...]
                ref[y, end + own] = mean_ref[...]
                ref[y, end + other] = jnp.zeros((8, 128), f32)


def merge(*refs):
    parts, out_ref = refs[:-1], refs[-1]
    for q, blocks in enumerate(PARTS):
        keep, other = parts[2 * q:2 * q + 2]
        for n, (row, col) in enumerate(blocks):
            for y in range(4):
                for zl in range(4):
                    at, to = n * 8 + zl * 2, zl * 8 + col * 2
                    out_ref[row * 4 + y, to:to + 2] = keep[y, at:at + 2] + other[y, at:at + 2]
    keep, other = parts[-2:]
    end = len(PARTS[-1]) * 8
    for x in range(4):
        for y in range(4):
            out_ref[x * 4 + y, 32:35] = keep[y, end:end + 3] + other[y, end:end + 3]


def between(shift_ref, select):
    wide = jnp.concatenate([shift_ref[cb] for cb in range(8)], axis=1)
    rows = [
        lax.dot_general(one_hot, shift_ref[block], NT, precision=HI, preferred_element_type=f32)
        for block, one_hot in select
    ]
    rows = jnp.concatenate(rows, axis=0) if len(rows) > 1 else rows[0]
    return jnp.dot(rows, wide, precision=HI, preferred_element_type=f32)


def fold(part_ref, out_ref, shift_ref):
    x, y, c = lax.axis_index("x"), lax.axis_index("y"), lax.axis_index("c")
    sub = lax.broadcasted_iota(jnp.int32, (8, 128), 0)
    lane = lax.broadcasted_iota(jnp.int32, (8, 128), 1)

    def summed(t):
        s = part_ref[0, t]
        for p in range(1, 16):
            s = s + part_ref[p, t]
        return s

    mean = (summed(33) + summed(34)) * f32(1.0 / 32)
    spread = summed(32)
    for k in range(2):
        for p in range(16):
            shift = part_ref[p, 33 + k] - mean
            spread = spread + shift * shift * f32(TILE)
            for cb in range(8):
                shift_ref[cb, k * 16 + p:k * 16 + p + 1, :] = shift[cb:cb + 1]
    select = []
    for zl in range(4):
        want = (zl % 2) * 64 + y * 16 + (sub // 4) * 8 + c * 4 + sub % 4
        select.append((2 * x + zl // 2, jnp.where(lane == want, f32(1), f32(0))))
    extra = between(shift_ref, select) * f32(TILE)
    for zl in range(4):
        for k in range(4):
            a, b = [
                summed(zl * 8 + cb) + extra[zl * 8:zl * 8 + 8, cb * 128:(cb + 1) * 128] for cb in (2 * k, 2 * k + 1)
            ]
            out_ref[zl * 2, k] = jnp.where(sub < 4, a, pltpu.roll(b, 4, 0))
            out_ref[zl * 2 + 1, k] = jnp.where(sub < 4, pltpu.roll(a, 4, 0), b)
        for zh in range(2):
            out_ref[zl * 2 + zh, 4] = spread
            out_ref[zl * 2 + zh, 5] = mean


def finish(part_ref, out_ref, shift_ref):
    first_row = lax.axis_index(AXES) * 4
    sub = lax.broadcasted_iota(jnp.int32, (8, 128), 0)
    lane = lax.broadcasted_iota(jnp.int32, (8, 128), 1)

    def summed(t):
        s = part_ref[0, t]
        for p in range(1, 8):
            s = s + part_ref[p, t]
        return s

    mean = summed(5) * f32(1.0 / 8)
    spread = summed(4)
    for p in range(8):
        shift = part_ref[p, 5] - mean
        spread = spread + shift * shift * f32(32 * TILE)
        for cb in range(8):
            shift_ref[cb, p:p + 1, :] = shift[cb:cb + 1]
    one_hot = jnp.where(lane == first_row % 128 + sub % 4, f32(1), f32(0))
    extra = between(shift_ref, [(first_row // 128, one_hot)]) * f32(32 * TILE)
    scale = 1.0 / jnp.sqrt(spread + 1e-06)
    flat = sub * 128 + lane
    own = jnp.zeros((8, 128), f32)
    for i in range(4):
        value = jnp.sum(jnp.where(flat == first_row + i, scale, 0.0))
        own = jnp.where((sub & 3) == i, value, own)
    for k in range(4):
        at, to = 2 * k * 128, (2 * k + 1) * 128
        cols = jnp.where(sub < 4, scale[2 * k:2 * k + 1, :], scale[2 * k + 1:2 * k + 2, :])
        more = jnp.where(sub < 4, extra[:, at:to], extra[:, to:to + 128])
        tile = (summed(k) + more) * cols * own
        out_ref[:, at:to] = tile[0:4]
        out_ref[:, to:to + 128] = tile[4:8]


def local(images):
    shape = jax.ShapeDtypeStruct
    vmem = pl.BlockSpec(memory_space=pltpu.VMEM)
    anywhere = pl.BlockSpec(memory_space=pl.ANY)
    params = pltpu.CompilerParams(vmem_limit_bytes=48 * 1024 * 1024)
    by_group = images.reshape(4, 2048, 128)
    by_eighth = images.reshape(8, 1024, 128)
    up = [(i, i + 1) for i in range(15)]
    down = [(j, i) for i, j in up]
    edge_shape = [shape((256, 128), f32)] * 2

    def unit_shape(count):
        return [shape((count, 1024), jnp.bfloat16), shape((1, count), f32), shape((1, count), f32)]

    def swap(axes, ahead, back):
        return lax.ppermute(ahead, axes, up), lax.ppermute(back, axes, down)

    left, right = pl.pallas_call(
        survey,
        grid=(4,),
        in_specs=[pl.BlockSpec((4, 512, 128), lambda i: (0, i, 0))],
        out_specs=[pl.BlockSpec((64, 128), lambda i: (i, 0))] * 2,
        out_shape=edge_shape,
        compiler_params=params,
    )(by_group)
    edges = swap(GY, right, left)
    weights = pl.pallas_call(
        build_weights,
        in_specs=[anywhere],
        out_specs=vmem,
        out_shape=shape((8, 256, 128), f32),
        compiler_params=params,
    )(left)

    def smooth_rows(group, count, order):
        top, bot = pl.pallas_call(
            functools.partial(row_pass, group, count),
            in_specs=[vmem] * 4 + [anywhere],
            out_specs=[vmem] * 2,
            out_shape=[shape((4, 256 * count, 128), f32)] * 2,
            compiler_params=params,
        )(by_eighth, *edges, weights, order)
        above, below = swap(GX, bot, top)
        return above, top, bot, below

    chunks = []
    for group, count in [(0, 1), (1, 1), (2, 1), (3, 1)]:
        chunks.append(smooth_rows(group, count, chunks[-1][1] if chunks else left))
    units, spreads, means, parts = [], [], [], []
    order = [left]
    for q, sources in enumerate(chunks):
        unit, spread, mean = pl.pallas_call(
            column_pass,
            in_specs=[vmem] * 4 + [anywhere] * len(order),
            out_specs=[vmem] * 3,
            out_shape=unit_shape(256),
            scratch_shapes=[pltpu.VMEM((256, 128), f32)] * 2,
            compiler_params=params,
        )(*sources, *order)
        units.append(unit)
        spreads.append(spread)
        means.append(mean)
        order = [unit]
        if q == 0:
            continue
        blocks = PARTS[q - 1]
        vectors = []
        if q == 3:
            vectors = [jnp.concatenate(v, axis=1).reshape(8, 128) for v in (spreads, means)]
        tiles = len(blocks) * 8 + (3 if vectors else 0)
        keep, send = pl.pallas_call(
            functools.partial(gram, blocks),
            in_specs=[vmem] * (len(units) + len(vectors)),
            out_specs=[vmem] * 2,
            out_shape=[shape((4, tiles, 8, 128), f32)] * 2,
            compiler_params=params,
        )(*units, *vectors)
        parts += [keep, lax.ppermute(send, "c", [(0, 1), (1, 0)])]
        order = [keep, parts[1]] if q == 2 else [keep]

    part = pl.pallas_call(
        merge,
        in_specs=[vmem] * 6,
        out_specs=vmem,
        out_shape=shape((16, 35, 8, 128), f32),
        compiler_params=params,
    )(*parts)
    part = lax.all_to_all(part, ("x", "y"), 0, 0, tiled=True)
    part = pl.pallas_call(
        fold,
        in_specs=[vmem],
        out_specs=vmem,
        out_shape=shape((8, 6, 8, 128), f32),
        scratch_shapes=[pltpu.VMEM((8, 32, 128), f32)],
        compiler_params=params,
    )(part)
    part = lax.all_to_all(part, ("zl", "zh"), 0, 0, tiled=True)
    return pl.pallas_call(
        finish,
        in_specs=[vmem],
        out_specs=vmem,
        out_shape=shape((4, 1024), f32),
        scratch_shapes=[pltpu.VMEM((8, 8, 128), f32)],
        compiler_params=params,
    )(part)


def solution(mesh):
    fine = Mesh(mesh.devices.reshape(4, 4, 4, 2, 2), AXES)
    return jax.shard_map(
        local,
        mesh=fine,
        in_specs=(P(None, GX, GY),),
        out_specs=P(AXES, None),
        check_vma=False,
    )
```

```python
import functools
import math

import jax
import jax.numpy as jnp
from jax import lax
from jax.experimental import pallas as pl
from jax.experimental.pallas import tpu as pltpu
from jax.sharding import Mesh, PartitionSpec as P

f32 = jnp.float32
HI = lax.Precision.HIGHEST
NT = (((1,), (1,)), ((), ()))
TILE = 8 * 128
PARTS = (
    ((0, 0), (0, 1), (1, 0), (1, 1)),
    ((2, 0), (2, 1), (2, 2), (0, 2), (1, 2)),
    ((3, 0), (3, 1), (3, 2), (3, 3), (0, 3), (1, 3), (2, 3)),
)
GX, GY = ("x", "zl"), ("y", "zh", "c")
AXES = GX + GY


def stencil_taps():
    raw = [math.exp(-k * k / 4.5) for k in range(-4, 5)]
    total = sum(raw)
    return [value / total for value in raw]


TAPS = stencil_taps()


def survey(x_ref, left_ref, right_ref):
    lane = lax.broadcasted_iota(jnp.int32, (64, 128), 1)
    left = jnp.zeros((64, 128), f32)
    right = jnp.zeros((64, 128), f32)
    for g in range(4):
        for r in range(8):
            row = x_ref[g, pl.ds(r, 64, stride=8), :]
            slot = g * 32 + r * 4
            here = (lane >= slot) & (lane < slot + 4)
            left = jnp.where(here, pltpu.roll(row, slot, 1) if slot else row, left)
            right = jnp.where(here, pltpu.roll(row, (slot + 4) % 128, 1), right)
    left_ref[...] = left
    right_ref[...] = right


def build_weights(order_ref, w_ref):
    at = lax.broadcasted_iota(jnp.int32, (128, 128), 0)
    col = lax.broadcasted_iota(jnp.int32, (128, 128), 1)

    def taps(distance):
        value = jnp.zeros((128, 128), f32)
        for k in range(5):
            value = jnp.where(distance == k, f32(TAPS[4 + k]), value)
        return value

    band = taps(jnp.abs(at - col))
    halo = taps(jnp.abs(at % 4 + jnp.where(at < 32, -4, 128) - col))
    for r in range(8):
        w_ref[r, 0:128] = band
        w_ref[r, 128:256] = jnp.where((at < 64) & (at % 32 // 4 == r), halo, 0.0)


def halo_lanes(g, left, right):
    lane = lax.broadcasted_iota(jnp.int32, left.shape, 1)
    left = pltpu.roll(left, (128 - 32 * g) % 128, 1) if g else left
    right = pltpu.roll(right, (160 - 32 * g) % 128, 1) if g != 1 else right
    return jnp.where(lane < 32, left, jnp.where(lane < 64, right, 0.0))


def smooth_row(row, halo, w):
    wide = jnp.concatenate([row, halo], axis=1)
    return jnp.dot(wide, w, precision=HI, preferred_element_type=f32)


def row_pass(start, count, x_ref, left_ref, right_ref, w_ref, order_ref, top_ref, bot_ref):
    for part in range(count):
        at = slice(part * 128, (part + 1) * 128)
        group, half = divmod(start + part, 2)
        edge = slice(half * 128, half * 128 + 128)
        halo = halo_lanes(group, left_ref[edge], right_ref[edge])
        for r in range(8):
            smooth = smooth_row(x_ref[part, pl.ds(r, 128, stride=8), :], halo, w_ref[r])
            if r < 4:
                top_ref[r, at] = smooth
            else:
                bot_ref[r - 4, at] = smooth


def to_lanes(squares, level):
    ones = jnp.ones((8, 128), f32)
    pick = jnp.where(lax.broadcasted_iota(jnp.int32, (8, 128), 1) == 0, f32(1), f32(0))
    spread = lax.dot_general(ones, squares, NT, precision=HI, preferred_element_type=f32)
    mean = lax.dot_general(pick, level, NT, precision=HI, preferred_element_type=f32)
    return spread[0:1], mean[0:1]


def smooth_down(rows):
    smooth = []
    for r in range(8):
        v = rows[r + 4] * TAPS[4]
        for k in range(1, 5):
            v = v + (rows[r + 4 - k] + rows[r + 4 + k]) * TAPS[4 + k]
        smooth.append(v)
    return smooth


def column_pass(above_ref, top_ref, bot_ref, below_ref, *refs):
    u_ref, spread_ref, mean_ref, square_ref, level_ref = refs[-5:]

    def step(s, carry):
        at = pl.ds(pl.multiple_of(s * 16, 16), 16)
        smooth = smooth_down([ref[i, at, :] for ref in (above_ref, top_ref, bot_ref, below_ref) for i in range(4)])
        total = ((smooth[0] + smooth[1]) + (smooth[2] + smooth[3])) + ((smooth[4] + smooth[5]) + (smooth[6] + smooth[7]))
        mean = jnp.sum(total, axis=1, keepdims=True) * f32(1.0 / TILE)
        acc = jnp.zeros((16, 128), f32)
        for r in range(8):
            centered = smooth[r] - mean
            acc = acc + centered * centered
            u_ref[at, r * 128:(r + 1) * 128] = centered.astype(jnp.bfloat16)
        square_ref[at, :] = acc
        level_ref[at, :] = jnp.broadcast_to(mean, (16, 128))
        return carry

    lax.fori_loop(0, square_ref.shape[0] // 16, step, 0, unroll=4)
    spread_ref[...], mean_ref[...] = to_lanes(square_ref[...], level_ref[...])


def gram(blocks, pieces, *refs):
    count = 1 + max(a for a, b in blocks)
    units, refs = refs[:count], refs[count:]
    vectors, keep_ref, sends = refs[:-1 - pieces], refs[-1 - pieces], refs[-pieces:]
    each = len(blocks) * 8 // pieces if pieces > 1 else sends[0].shape[1]
    first = lax.axis_index("c") == 0
    sub = lax.broadcasted_iota(jnp.int32, (8, 128), 0)
    for n, (row, col) in enumerate(blocks):
        part = lax.dot_general(units[row][...], units[col][...], NT, preferred_element_type=f32)
        for zl in range(4):
            for y in range(4):
                at = (zl * 4 + y) * 16
                for cb in range(2):
                    a = part[at:at + 8, cb * 128:(cb + 1) * 128]
                    b = part[at + 8:at + 16, cb * 128:(cb + 1) * 128]
                    c0 = jnp.where(sub < 4, a, pltpu.roll(b, 4, 0))
                    c1 = jnp.where(sub < 4, pltpu.roll(a, 4, 0), b)
                    keep_ref[y, n * 8 + zl * 2 + cb] = jnp.where(first, c0, c1)
                    tile = n * 8 + zl * 2 + cb
                    sends[tile // each][y, tile % each] = jnp.where(first, c1, c0)
    if vectors:
        spread_ref, mean_ref = vectors[:2]
        end = len(blocks) * 8
        for y in range(4):
            for ref, own, other in ((keep_ref, 1, 2), (sends[0], 2, 1)):
                ref[y, end] = spread_ref[...]
                ref[y, end + own] = mean_ref[...]
                ref[y, end + other] = jnp.zeros((8, 128), f32)


def by_turn(early_ref, early_other_ref, late_ref, *refs):
    others, outs = refs[:-4], refs[-4:]
    y = lax.axis_index("y")
    start = early_ref.shape[1]
    each = late_ref.shape[1] // len(others)
    for turn, ref in enumerate(outs):
        to = (y + turn) % 4
        ref[:start] = early_ref[to] + early_other_ref[to]
        for n, other in enumerate(others):
            ref[start + n * each:start + (n + 1) * each] = late_ref[to, n * each:(n + 1) * each] + other[to]


def add(*refs):
    refs[-1][...] = refs[0][...] + refs[1][...]


def regroup(*refs):
    last, out_ref = refs[-2:]
    for q, blocks in enumerate(PARTS):
        turns = refs[0:4] if q < 2 else [last.at[y] for y in range(4)]
        start = len(PARTS[0]) * 8 if q == 1 else 0
        for n, (row, col) in enumerate(blocks):
            for zl in range(4):
                at, to = start + n * 8 + zl * 2, zl * 8 + col * 2
                a, b, c, d = [ref[at:at + 2] for ref in turns]
                out_ref[row, to:to + 2] = (a + b) + (c + d)
    end = len(PARTS[-1]) * 8
    spread = (last[0, end] + last[1, end]) + (last[2, end] + last[3, end])
    for x in range(4):
        out_ref[x, 32] = spread
        for y in range(4):
            out_ref[x, 33 + 2 * y:35 + 2 * y] = last[y, end + 1:end + 3]


def between(shift_ref, select):
    wide = jnp.concatenate([shift_ref[cb] for cb in range(8)], axis=1)
    rows = [
        lax.dot_general(one_hot, shift_ref[block], NT, precision=HI, preferred_element_type=f32)
        for block, one_hot in select
    ]
    rows = jnp.concatenate(rows, axis=0) if len(rows) > 1 else rows[0]
    return jnp.dot(rows, wide, precision=HI, preferred_element_type=f32)


def fold(part_ref, out_ref, shift_ref):
    x, y, c = lax.axis_index("x"), lax.axis_index("y"), lax.axis_index("c")
    sub = lax.broadcasted_iota(jnp.int32, (8, 128), 0)
    lane = lax.broadcasted_iota(jnp.int32, (8, 128), 1)

    def summed(t):
        return (part_ref[0, t] + part_ref[1, t]) + (part_ref[2, t] + part_ref[3, t])

    mean = summed(33)
    for k in range(1, 8):
        mean = mean + summed(33 + k)
    mean = mean * f32(1.0 / 32)
    spread = summed(32)
    for k in range(8):
        for p in range(4):
            shift = part_ref[p, 33 + k] - mean
            spread = spread + shift * shift * f32(TILE)
            for cb in range(8):
                shift_ref[cb, k * 4 + p:k * 4 + p + 1, :] = shift[cb:cb + 1]
    select = []
    for zl in range(4):
        want = (zl % 2) * 64 + y * 16 + (sub // 4) * 8 + c * 4 + sub % 4
        select.append((2 * x + zl // 2, jnp.where(lane == want, f32(1), f32(0))))
    extra = between(shift_ref, select) * f32(TILE)
    for zl in range(4):
        for k in range(4):
            a, b = [
                summed(zl * 8 + cb) + extra[zl * 8:zl * 8 + 8, cb * 128:(cb + 1) * 128] for cb in (2 * k, 2 * k + 1)
            ]
            out_ref[zl * 2, k] = jnp.where(sub < 4, a, pltpu.roll(b, 4, 0))
            out_ref[zl * 2 + 1, k] = jnp.where(sub < 4, pltpu.roll(a, 4, 0), b)
        for zh in range(2):
            out_ref[zl * 2 + zh, 4] = spread
            out_ref[zl * 2 + zh, 5] = mean


def finish(part_ref, out_ref, shift_ref):
    first_row = lax.axis_index(AXES) * 4
    sub = lax.broadcasted_iota(jnp.int32, (8, 128), 0)
    lane = lax.broadcasted_iota(jnp.int32, (8, 128), 1)

    def summed(t):
        s = part_ref[0, t]
        for p in range(1, 8):
            s = s + part_ref[p, t]
        return s

    mean = summed(5) * f32(1.0 / 8)
    spread = summed(4)
    for p in range(8):
        shift = part_ref[p, 5] - mean
        spread = spread + shift * shift * f32(32 * TILE)
        for cb in range(8):
            shift_ref[cb, p:p + 1, :] = shift[cb:cb + 1]
    one_hot = jnp.where(lane == first_row % 128 + sub % 4, f32(1), f32(0))
    extra = between(shift_ref, [(first_row // 128, one_hot)]) * f32(32 * TILE)
    scale = 1.0 / jnp.sqrt(spread + 1e-06)
    flat = sub * 128 + lane
    own = jnp.zeros((8, 128), f32)
    for i in range(4):
        value = jnp.sum(jnp.where(flat == first_row + i, scale, 0.0))
        own = jnp.where((sub & 3) == i, value, own)
    for k in range(4):
        at, to = 2 * k * 128, (2 * k + 1) * 128
        cols = jnp.where(sub < 4, scale[2 * k:2 * k + 1, :], scale[2 * k + 1:2 * k + 2, :])
        more = jnp.where(sub < 4, extra[:, at:to], extra[:, to:to + 128])
        tile = (summed(k) + more) * cols * own
        out_ref[:, at:to] = tile[0:4]
        out_ref[:, to:to + 128] = tile[4:8]


def local(images):
    shape = jax.ShapeDtypeStruct
    vmem = pl.BlockSpec(memory_space=pltpu.VMEM)
    anywhere = pl.BlockSpec(memory_space=pl.ANY)
    params = pltpu.CompilerParams(vmem_limit_bytes=48 * 1024 * 1024)
    by_group = images.reshape(4, 2048, 128)
    by_eighth = images.reshape(8, 1024, 128)
    up = [(i, i + 1) for i in range(15)]
    down = [(j, i) for i, j in up]
    edge_shape = [shape((256, 128), f32)] * 2

    def unit_shape(count):
        return [shape((count, 1024), jnp.bfloat16), shape((1, count), f32), shape((1, count), f32)]

    def swap(axes, ahead, back):
        return lax.ppermute(ahead, axes, up), lax.ppermute(back, axes, down)

    left, right = pl.pallas_call(
        survey,
        grid=(4,),
        in_specs=[pl.BlockSpec((4, 512, 128), lambda i: (0, i, 0))],
        out_specs=[pl.BlockSpec((64, 128), lambda i: (i, 0))] * 2,
        out_shape=edge_shape,
        compiler_params=pltpu.CompilerParams(vmem_limit_bytes=60 * 1024 * 1024),
    )(by_group)
    edges = swap(GY, right, left)
    weights = pl.pallas_call(
        build_weights,
        in_specs=[anywhere],
        out_specs=vmem,
        out_shape=shape((8, 256, 128), f32),
        compiler_params=params,
    )(left)

    def smooth_rows(start, count, order):
        top, bot = pl.pallas_call(
            functools.partial(row_pass, start, count),
            grid=(1,),
            in_specs=[pl.BlockSpec((count, 1024, 128), lambda i: (start // count, 0, 0))] + [vmem] * 3 + [anywhere],
            out_specs=[vmem] * 2,
            out_shape=[shape((4, 128 * count, 128), f32)] * 2,
            compiler_params=params,
        )(by_eighth, *edges, weights, order)
        above, below = swap(GX, bot, top)
        return above, top, bot, below

    def columns(sources, order):
        count = sources[0].shape[1]
        return pl.pallas_call(
            column_pass,
            in_specs=[vmem] * 4 + [anywhere] * len(order),
            out_specs=[vmem] * 3,
            out_shape=unit_shape(count),
            scratch_shapes=[pltpu.VMEM((count, 128), f32)] * 2,
            compiler_params=params,
        )(*sources, *order)

    def multiply(blocks, pieces, *operands):
        tiles = len(blocks) * 8 + (3 if len(operands) > 4 else 0)
        keep, *send = pl.pallas_call(
            functools.partial(gram, blocks, pieces),
            in_specs=([vmem] * 6 + [anywhere] * 4)[:len(operands)],
            out_specs=[vmem] * (1 + pieces),
            out_shape=[shape((4, tiles, 8, 128), f32)] + [shape((4, tiles // pieces, 8, 128), f32)] * pieces,
            compiler_params=params,
        )(*operands)
        return [keep] + [lax.ppermute(piece, "c", [(0, 1), (1, 0)]) for piece in send]

    chunks = []
    for start in (0, 2, 4, 6):
        chunks.append(smooth_rows(start, 2, chunks[-1][1] if chunks else left))
    results = [columns(chunks[0], [chunks[3][1]])]
    results.append(columns(chunks[1], [results[0][0]]))
    early = multiply(PARTS[0], 1, *[result[0] for result in results])
    results.append(columns(chunks[2], [early[0]]))
    late = multiply(PARTS[1], 8, *[result[0] for result in results])
    turns = pl.pallas_call(
        by_turn,
        in_specs=[vmem] * (3 + 8),
        out_specs=[vmem] * 4,
        out_shape=[shape((72, 8, 128), f32)] * 4,
        compiler_params=params,
    )(*early, *late)
    moved = [lax.ppermute(turns[k], "y", [(i, (i + k) % 4) for i in range(4)]) for k in range(1, 4)]
    results.append(columns(chunks[3], [turns[0]]))
    units, spreads, means = zip(*results)
    vectors = [jnp.concatenate(v, axis=1).reshape(8, 128) for v in (spreads, means)]
    keep, other = multiply(PARTS[2], 1, *units, *vectors, *moved)
    last = pl.pallas_call(
        add,
        in_specs=[vmem] * 2,
        out_specs=vmem,
        out_shape=shape(keep.shape, f32),
        compiler_params=params,
    )(keep, other)
    parts = [turns[0]] + moved + [lax.all_to_all(last, "y", 0, 0, tiled=True)]

    part = pl.pallas_call(
        regroup,
        in_specs=[vmem] * 5,
        out_specs=vmem,
        out_shape=shape((4, 41, 8, 128), f32),
        compiler_params=params,
    )(*parts)
    part = lax.all_to_all(part, "x", 0, 0, tiled=True)
    part = pl.pallas_call(
        fold,
        in_specs=[vmem],
        out_specs=vmem,
        out_shape=shape((8, 6, 8, 128), f32),
        scratch_shapes=[pltpu.VMEM((8, 32, 128), f32)],
        compiler_params=params,
    )(part)
    part = lax.all_to_all(part, ("zl", "zh"), 0, 0, tiled=True)
    return pl.pallas_call(
        finish,
        in_specs=[vmem],
        out_specs=vmem,
        out_shape=shape((4, 1024), f32),
        scratch_shapes=[pltpu.VMEM((8, 8, 128), f32)],
        compiler_params=params,
    )(part)


def solution(mesh):
    fine = Mesh(mesh.devices.reshape(4, 4, 4, 2, 2), AXES)
    return jax.shard_map(
        local,
        mesh=fine,
        in_specs=(P(None, GX, GY),),
        out_specs=P(AXES, None),
        check_vma=False,
    )
```

```python
import functools
import math

import jax
import jax.numpy as jnp
from jax import lax
from jax.experimental import pallas as pl
from jax.experimental.pallas import tpu as pltpu
from jax.sharding import Mesh, PartitionSpec as P

f32 = jnp.float32
HI = lax.Precision.HIGHEST
NT = (((1,), (1,)), ((), ()))
TILE = 8 * 128
PARTS = (
    ((0, 0), (0, 1), (1, 0), (1, 1)),
    ((2, 0), (2, 1), (0, 2)),
    ((3, 0), (3, 1), (3, 2), (3, 3), (0, 3), (1, 3), (2, 3), (2, 2), (1, 2)),
)
GX, GY = ("x", "zl"), ("y", "zh", "c")
AXES = GX + GY


def stencil_taps():
    raw = [math.exp(-k * k / 4.5) for k in range(-4, 5)]
    total = sum(raw)
    return [value / total for value in raw]


TAPS = stencil_taps()


def survey(x_ref, left_ref, right_ref):
    lane = lax.broadcasted_iota(jnp.int32, (64, 128), 1)
    left = jnp.zeros((64, 128), f32)
    right = jnp.zeros((64, 128), f32)
    for g in range(4):
        for r in range(8):
            row = x_ref[g, pl.ds(r, 64, stride=8), :]
            slot = g * 32 + r * 4
            here = (lane >= slot) & (lane < slot + 4)
            left = jnp.where(here, pltpu.roll(row, slot, 1) if slot else row, left)
            right = jnp.where(here, pltpu.roll(row, (slot + 4) % 128, 1), right)
    left_ref[...] = left
    right_ref[...] = right


def build_weights(order_ref, w_ref):
    at = lax.broadcasted_iota(jnp.int32, (128, 128), 0)
    col = lax.broadcasted_iota(jnp.int32, (128, 128), 1)

    def taps(distance):
        value = jnp.zeros((128, 128), f32)
        for k in range(5):
            value = jnp.where(distance == k, f32(TAPS[4 + k]), value)
        return value

    band = taps(jnp.abs(at - col))
    halo = taps(jnp.abs(at % 4 + jnp.where(at < 32, -4, 128) - col))
    for r in range(8):
        w_ref[r, 0:128] = band
        w_ref[r, 128:256] = jnp.where((at < 64) & (at % 32 // 4 == r), halo, 0.0)


def halo_lanes(g, left, right):
    lane = lax.broadcasted_iota(jnp.int32, left.shape, 1)
    left = pltpu.roll(left, (128 - 32 * g) % 128, 1) if g else left
    right = pltpu.roll(right, (160 - 32 * g) % 128, 1) if g != 1 else right
    return jnp.where(lane < 32, left, jnp.where(lane < 64, right, 0.0))


def smooth_row(row, halo, w):
    wide = jnp.concatenate([row, halo], axis=1)
    return jnp.dot(wide, w, precision=HI, preferred_element_type=f32)


def row_pass(start, count, x_ref, left_ref, right_ref, w_ref, order_ref, top_ref, bot_ref):
    for part in range(count):
        at = slice(part * 128, (part + 1) * 128)
        group, half = divmod(start + part, 2)
        edge = slice(half * 128, half * 128 + 128)
        halo = halo_lanes(group, left_ref[edge], right_ref[edge])
        for r in range(8):
            smooth = smooth_row(x_ref[part, pl.ds(r, 128, stride=8), :], halo, w_ref[r])
            if r < 4:
                top_ref[r, at] = smooth
            else:
                bot_ref[r - 4, at] = smooth


def to_lanes(squares, level):
    ones = jnp.ones((8, 128), f32)
    pick = jnp.where(lax.broadcasted_iota(jnp.int32, (8, 128), 1) == 0, f32(1), f32(0))
    spread = lax.dot_general(ones, squares, NT, precision=HI, preferred_element_type=f32)
    mean = lax.dot_general(pick, level, NT, precision=HI, preferred_element_type=f32)
    return spread[0:1], mean[0:1]


def smooth_down(rows):
    smooth = []
    for r in range(8):
        v = rows[r + 4] * TAPS[4]
        for k in range(1, 5):
            v = v + (rows[r + 4 - k] + rows[r + 4 + k]) * TAPS[4 + k]
        smooth.append(v)
    return smooth


def column_pass(above_ref, top_ref, bot_ref, below_ref, *refs):
    u_ref, spread_ref, mean_ref, square_ref, level_ref = refs[-5:]

    def step(s, carry):
        at = pl.ds(pl.multiple_of(s * 16, 16), 16)
        smooth = smooth_down([ref[i, at, :] for ref in (above_ref, top_ref, bot_ref, below_ref) for i in range(4)])
        total = ((smooth[0] + smooth[1]) + (smooth[2] + smooth[3])) + ((smooth[4] + smooth[5]) + (smooth[6] + smooth[7]))
        mean = jnp.sum(total, axis=1, keepdims=True) * f32(1.0 / TILE)
        acc = jnp.zeros((16, 128), f32)
        for r in range(8):
            centered = smooth[r] - mean
            acc = acc + centered * centered
            u_ref[at, r * 128:(r + 1) * 128] = centered.astype(jnp.bfloat16)
        square_ref[at, :] = acc
        level_ref[at, :] = jnp.broadcast_to(mean, (16, 128))
        return carry

    lax.fori_loop(0, square_ref.shape[0] // 16, step, 0, unroll=4)
    spread_ref[...], mean_ref[...] = to_lanes(square_ref[...], level_ref[...])


def gram(blocks, pieces, *refs):
    count = 1 + max(a for a, b in blocks)
    units, refs = refs[:count], refs[count:]
    vectors, keep_ref, sends = refs[:-1 - pieces], refs[-1 - pieces], refs[-pieces:]
    each = len(blocks) * 8 // pieces if pieces > 1 else sends[0].shape[1]
    first = lax.axis_index("c") == 0
    sub = lax.broadcasted_iota(jnp.int32, (8, 128), 0)
    for n, (row, col) in enumerate(blocks):
        part = lax.dot_general(units[row][...], units[col][...], NT, preferred_element_type=f32)
        for zl in range(4):
            for y in range(4):
                at = (zl * 4 + y) * 16
                for cb in range(2):
                    a = part[at:at + 8, cb * 128:(cb + 1) * 128]
                    b = part[at + 8:at + 16, cb * 128:(cb + 1) * 128]
                    c0 = jnp.where(sub < 4, a, pltpu.roll(b, 4, 0))
                    c1 = jnp.where(sub < 4, pltpu.roll(a, 4, 0), b)
                    keep_ref[y, n * 8 + zl * 2 + cb] = jnp.where(first, c0, c1)
                    tile = n * 8 + zl * 2 + cb
                    sends[tile // each][y, tile % each] = jnp.where(first, c1, c0)
    if vectors:
        spread_ref, mean_ref = vectors[:2]
        end = len(blocks) * 8
        for y in range(4):
            for ref, own, other in ((keep_ref, 1, 2), (sends[0], 2, 1)):
                ref[y, end] = spread_ref[...]
                ref[y, end + own] = mean_ref[...]
                ref[y, end + other] = jnp.zeros((8, 128), f32)


def by_turn(early_ref, early_other_ref, late_ref, *refs):
    others, outs = refs[:-4], refs[-4:]
    y = lax.axis_index("y")
    start = early_ref.shape[1]
    each = late_ref.shape[1] // len(others)
    for turn, ref in enumerate(outs):
        to = (y + turn) % 4
        ref[:start] = early_ref[to] + early_other_ref[to]
        for n, other in enumerate(others):
            ref[start + n * each:start + (n + 1) * each] = late_ref[to, n * each:(n + 1) * each] + other[to]


def add(*refs):
    refs[-1][...] = refs[0][...] + refs[1][...]


def regroup(*refs):
    last, out_ref = refs[-2:]
    for q, blocks in enumerate(PARTS):
        turns = refs[0:4] if q < 2 else [last.at[y] for y in range(4)]
        start = len(PARTS[0]) * 8 if q == 1 else 0
        for n, (row, col) in enumerate(blocks):
            for zl in range(4):
                at, to = start + n * 8 + zl * 2, zl * 8 + col * 2
                a, b, c, d = [ref[at:at + 2] for ref in turns]
                out_ref[row, to:to + 2] = (a + b) + (c + d)
    end = len(PARTS[-1]) * 8
    spread = (last[0, end] + last[1, end]) + (last[2, end] + last[3, end])
    for x in range(4):
        out_ref[x, 32] = spread
        for y in range(4):
            out_ref[x, 33 + 2 * y:35 + 2 * y] = last[y, end + 1:end + 3]


def between(shift_ref, select):
    wide = jnp.concatenate([shift_ref[cb] for cb in range(8)], axis=1)
    rows = [
        lax.dot_general(one_hot, shift_ref[block], NT, precision=HI, preferred_element_type=f32)
        for block, one_hot in select
    ]
    rows = jnp.concatenate(rows, axis=0) if len(rows) > 1 else rows[0]
    return jnp.dot(rows, wide, precision=HI, preferred_element_type=f32)


def fold(part_ref, out_ref, shift_ref):
    x, y, c = lax.axis_index("x"), lax.axis_index("y"), lax.axis_index("c")
    sub = lax.broadcasted_iota(jnp.int32, (8, 128), 0)
    lane = lax.broadcasted_iota(jnp.int32, (8, 128), 1)

    def summed(t):
        return (part_ref[0, t] + part_ref[1, t]) + (part_ref[2, t] + part_ref[3, t])

    mean = summed(33)
    for k in range(1, 8):
        mean = mean + summed(33 + k)
    mean = mean * f32(1.0 / 32)
    spread = summed(32)
    for k in range(8):
        for p in range(4):
            shift = part_ref[p, 33 + k] - mean
            spread = spread + shift * shift * f32(TILE)
            for cb in range(8):
                shift_ref[cb, k * 4 + p:k * 4 + p + 1, :] = shift[cb:cb + 1]
    select = []
    for zl in range(4):
        want = (zl % 2) * 64 + y * 16 + (sub // 4) * 8 + c * 4 + sub % 4
        select.append((2 * x + zl // 2, jnp.where(lane == want, f32(1), f32(0))))
    extra = between(shift_ref, select) * f32(TILE)
    for zl in range(4):
        for k in range(4):
            a, b = [
                summed(zl * 8 + cb) + extra[zl * 8:zl * 8 + 8, cb * 128:(cb + 1) * 128] for cb in (2 * k, 2 * k + 1)
            ]
            out_ref[zl * 2, k] = jnp.where(sub < 4, a, pltpu.roll(b, 4, 0))
            out_ref[zl * 2 + 1, k] = jnp.where(sub < 4, pltpu.roll(a, 4, 0), b)
        for zh in range(2):
            out_ref[zl * 2 + zh, 4] = spread
            out_ref[zl * 2 + zh, 5] = mean


def finish(part_ref, out_ref, shift_ref):
    first_row = lax.axis_index(AXES) * 4
    sub = lax.broadcasted_iota(jnp.int32, (8, 128), 0)
    lane = lax.broadcasted_iota(jnp.int32, (8, 128), 1)

    def summed(t):
        s = part_ref[0, t]
        for p in range(1, 8):
            s = s + part_ref[p, t]
        return s

    mean = summed(5) * f32(1.0 / 8)
    spread = summed(4)
    for p in range(8):
        shift = part_ref[p, 5] - mean
        spread = spread + shift * shift * f32(32 * TILE)
        for cb in range(8):
            shift_ref[cb, p:p + 1, :] = shift[cb:cb + 1]
    one_hot = jnp.where(lane == first_row % 128 + sub % 4, f32(1), f32(0))
    extra = between(shift_ref, [(first_row // 128, one_hot)]) * f32(32 * TILE)
    scale = 1.0 / jnp.sqrt(spread + 1e-06)
    flat = sub * 128 + lane
    own = jnp.zeros((8, 128), f32)
    for i in range(4):
        value = jnp.sum(jnp.where(flat == first_row + i, scale, 0.0))
        own = jnp.where((sub & 3) == i, value, own)
    for k in range(4):
        at, to = 2 * k * 128, (2 * k + 1) * 128
        cols = jnp.where(sub < 4, scale[2 * k:2 * k + 1, :], scale[2 * k + 1:2 * k + 2, :])
        more = jnp.where(sub < 4, extra[:, at:to], extra[:, to:to + 128])
        tile = (summed(k) + more) * cols * own
        out_ref[:, at:to] = tile[0:4]
        out_ref[:, to:to + 128] = tile[4:8]


def local(images):
    shape = jax.ShapeDtypeStruct
    vmem = pl.BlockSpec(memory_space=pltpu.VMEM)
    anywhere = pl.BlockSpec(memory_space=pl.ANY)
    params = pltpu.CompilerParams(vmem_limit_bytes=48 * 1024 * 1024)
    by_group = images.reshape(4, 2048, 128)
    by_eighth = images.reshape(8, 1024, 128)
    up = [(i, i + 1) for i in range(15)]
    down = [(j, i) for i, j in up]
    edge_shape = [shape((256, 128), f32)] * 2

    def unit_shape(count):
        return [shape((count, 1024), jnp.bfloat16), shape((1, count), f32), shape((1, count), f32)]

    def swap(axes, ahead, back):
        return lax.ppermute(ahead, axes, up), lax.ppermute(back, axes, down)

    left, right = pl.pallas_call(
        survey,
        grid=(4,),
        in_specs=[pl.BlockSpec((4, 512, 128), lambda i: (0, i, 0))],
        out_specs=[pl.BlockSpec((64, 128), lambda i: (i, 0))] * 2,
        out_shape=edge_shape,
        compiler_params=pltpu.CompilerParams(vmem_limit_bytes=60 * 1024 * 1024),
    )(by_group)
    edges = swap(GY, right, left)
    weights = pl.pallas_call(
        build_weights,
        in_specs=[anywhere],
        out_specs=vmem,
        out_shape=shape((8, 256, 128), f32),
        compiler_params=params,
    )(left)

    def smooth_rows(start, count, order):
        top, bot = pl.pallas_call(
            functools.partial(row_pass, start, count),
            grid=(1,),
            in_specs=[pl.BlockSpec((count, 1024, 128), lambda i: (start // count, 0, 0))] + [vmem] * 3 + [anywhere],
            out_specs=[vmem] * 2,
            out_shape=[shape((4, 128 * count, 128), f32)] * 2,
            compiler_params=params,
        )(by_eighth, *edges, weights, order)
        above, below = swap(GX, bot, top)
        return above, top, bot, below

    def columns(sources, order):
        count = sources[0].shape[1]
        return pl.pallas_call(
            column_pass,
            in_specs=[vmem] * 4 + [anywhere] * len(order),
            out_specs=[vmem] * 3,
            out_shape=unit_shape(count),
            scratch_shapes=[pltpu.VMEM((count, 128), f32)] * 2,
            compiler_params=params,
        )(*sources, *order)

    def multiply(blocks, pieces, *operands):
        tiles = len(blocks) * 8 + (3 if len(operands) > 4 else 0)
        keep, *send = pl.pallas_call(
            functools.partial(gram, blocks, pieces),
            in_specs=([vmem] * 6 + [anywhere] * 4)[:len(operands)],
            out_specs=[vmem] * (1 + pieces),
            out_shape=[shape((4, tiles, 8, 128), f32)] + [shape((4, tiles // pieces, 8, 128), f32)] * pieces,
            compiler_params=params,
        )(*operands)
        return [keep] + [lax.ppermute(piece, "c", [(0, 1), (1, 0)]) for piece in send]

    chunks = []
    for start in (0, 2, 4, 6):
        chunks.append(smooth_rows(start, 2, chunks[-1][1] if chunks else left))
    results = [columns(chunks[0], [chunks[3][1]])]
    results.append(columns(chunks[1], [results[0][0]]))
    early = multiply(PARTS[0], 1, *[result[0] for result in results])
    results.append(columns(chunks[2], [early[0]]))
    late = multiply(PARTS[1], 4, *[result[0] for result in results])
    turns = pl.pallas_call(
        by_turn,
        in_specs=[vmem] * (3 + 4),
        out_specs=[vmem] * 4,
        out_shape=[shape((56, 8, 128), f32)] * 4,
        compiler_params=params,
    )(*early, *late)
    moved = [lax.ppermute(turns[k], "y", [(i, (i + k) % 4) for i in range(4)]) for k in range(1, 4)]
    results.append(columns(chunks[3], [turns[0]]))
    units, spreads, means = zip(*results)
    vectors = [jnp.concatenate(v, axis=1).reshape(8, 128) for v in (spreads, means)]
    keep, other = multiply(PARTS[2], 1, *units, *vectors, *moved)
    last = pl.pallas_call(
        add,
        in_specs=[vmem] * 2,
        out_specs=vmem,
        out_shape=shape(keep.shape, f32),
        compiler_params=params,
    )(keep, other)
    parts = [turns[0]] + moved + [lax.all_to_all(last, "y", 0, 0, tiled=True)]

    part = pl.pallas_call(
        regroup,
        in_specs=[vmem] * 5,
        out_specs=vmem,
        out_shape=shape((4, 41, 8, 128), f32),
        compiler_params=params,
    )(*parts)
    part = lax.all_to_all(part, "x", 0, 0, tiled=True)
    part = pl.pallas_call(
        fold,
        in_specs=[vmem],
        out_specs=vmem,
        out_shape=shape((8, 6, 8, 128), f32),
        scratch_shapes=[pltpu.VMEM((8, 32, 128), f32)],
        compiler_params=params,
    )(part)
    part = lax.all_to_all(part, ("zl", "zh"), 0, 0, tiled=True)
    return pl.pallas_call(
        finish,
        in_specs=[vmem],
        out_specs=vmem,
        out_shape=shape((4, 1024), f32),
        scratch_shapes=[pltpu.VMEM((8, 8, 128), f32)],
        compiler_params=params,
    )(part)


def solution(mesh):
    fine = Mesh(mesh.devices.reshape(4, 4, 4, 2, 2), AXES)
    return jax.shard_map(
        local,
        mesh=fine,
        in_specs=(P(None, GX, GY),),
        out_specs=P(AXES, None),
        check_vma=False,
    )
```

```python
import functools
import math

import jax
import jax.numpy as jnp
from jax import lax
from jax.experimental import pallas as pl
from jax.experimental.pallas import tpu as pltpu
from jax.sharding import Mesh, PartitionSpec as P

f32 = jnp.float32
HI = lax.Precision.HIGHEST
NT = (((1,), (1,)), ((), ()))
TILE = 8 * 128
PARTS = (
    ((0, 0), (0, 1), (1, 0), (1, 1)),
    ((2, 0), (2, 1), (0, 2)),
    ((3, 0), (3, 1), (3, 2), (3, 3), (0, 3), (1, 3), (2, 3), (2, 2), (1, 2)),
)
GX, GY = ("x", "zl"), ("y", "zh", "c")
AXES = GX + GY


def stencil_taps():
    raw = [math.exp(-k * k / 4.5) for k in range(-4, 5)]
    total = sum(raw)
    return [value / total for value in raw]


TAPS = stencil_taps()


def survey(x_ref, left_ref, right_ref):
    lane = lax.broadcasted_iota(jnp.int32, (64, 128), 1)
    left = jnp.zeros((64, 128), f32)
    right = jnp.zeros((64, 128), f32)
    for g in range(4):
        for r in range(8):
            row = x_ref[g, pl.ds(r, 64, stride=8), :]
            slot = g * 32 + r * 4
            after = (slot + 4) % 128
            turned = pltpu.roll(row, after, 1) if after else row
            right = jnp.where((lane >= slot) & (lane < slot + 4), turned, right)
            left = jnp.where((lane >= after) & (lane < after + 4), turned, left)
    left_ref[...] = pltpu.roll(left, 124, 1)
    right_ref[...] = right


def build_weights(order_ref, w_ref):
    at = lax.broadcasted_iota(jnp.int32, (128, 128), 0)
    col = lax.broadcasted_iota(jnp.int32, (128, 128), 1)

    def taps(distance):
        value = jnp.zeros((128, 128), f32)
        for k in range(5):
            value = jnp.where(distance == k, f32(TAPS[4 + k]), value)
        return value

    band = taps(jnp.abs(at - col))
    halo = taps(jnp.abs(at % 4 + jnp.where(at < 32, -4, 128) - col))
    for r in range(8):
        w_ref[r, 0:128] = band
        w_ref[r, 128:256] = jnp.where((at < 64) & (at % 32 // 4 == r), halo, 0.0)


def halo_lanes(g, left, right):
    lane = lax.broadcasted_iota(jnp.int32, left.shape, 1)
    left = pltpu.roll(left, (128 - 32 * g) % 128, 1) if g else left
    right = pltpu.roll(right, (160 - 32 * g) % 128, 1) if g != 1 else right
    return jnp.where(lane < 32, left, jnp.where(lane < 64, right, 0.0))


def smooth_row(row, halo, w):
    wide = jnp.concatenate([row, halo], axis=1)
    return jnp.dot(wide, w, precision=HI, preferred_element_type=f32)


def row_pass(start, count, x_ref, left_ref, right_ref, w_ref, order_ref, top_ref, bot_ref):
    for part in range(count):
        at = slice(part * 128, (part + 1) * 128)
        group, half = divmod(start + part, 2)
        edge = slice(half * 128, half * 128 + 128)
        halo = halo_lanes(group, left_ref[edge], right_ref[edge])
        for r in range(8):
            smooth = smooth_row(x_ref[part, pl.ds(r, 128, stride=8), :], halo, w_ref[r])
            if r < 4:
                top_ref[r, at] = smooth
            else:
                bot_ref[r - 4, at] = smooth


def to_lanes(squares, level):
    ones = jnp.ones((8, 128), f32)
    pick = jnp.where(lax.broadcasted_iota(jnp.int32, (8, 128), 1) == 0, f32(1), f32(0))
    spread = lax.dot_general(ones, squares, NT, precision=HI, preferred_element_type=f32)
    mean = lax.dot_general(pick, level, NT, precision=HI, preferred_element_type=f32)
    return spread[0:1], mean[0:1]


def smooth_down(rows):
    smooth = []
    for r in range(8):
        v = rows[r + 4] * TAPS[4]
        for k in range(1, 5):
            v = v + (rows[r + 4 - k] + rows[r + 4 + k]) * TAPS[4 + k]
        smooth.append(v)
    return smooth


def column_pass(above_ref, top_ref, bot_ref, below_ref, *refs):
    u_ref, spread_ref, mean_ref, square_ref, level_ref = refs[-5:]

    def step(s, carry):
        at = pl.ds(pl.multiple_of(s * 16, 16), 16)
        smooth = smooth_down([ref[i, at, :] for ref in (above_ref, top_ref, bot_ref, below_ref) for i in range(4)])
        total = ((smooth[0] + smooth[1]) + (smooth[2] + smooth[3])) + ((smooth[4] + smooth[5]) + (smooth[6] + smooth[7]))
        mean = jnp.sum(total, axis=1, keepdims=True) * f32(1.0 / TILE)
        acc = jnp.zeros((16, 128), f32)
        for r in range(8):
            centered = smooth[r] - mean
            acc = acc + centered * centered
            u_ref[at, r * 128:(r + 1) * 128] = centered.astype(jnp.bfloat16)
        square_ref[at, :] = acc
        level_ref[at, :] = jnp.broadcast_to(mean, (16, 128))
        return carry

    lax.fori_loop(0, square_ref.shape[0] // 16, step, 0, unroll=4)
    spread_ref[...], mean_ref[...] = to_lanes(square_ref[...], level_ref[...])


def gram(blocks, pieces, *refs):
    count = 1 + max(a for a, b in blocks)
    units, refs = refs[:count], refs[count:]
    vectors, keep_ref, sends = refs[:-1 - pieces], refs[-1 - pieces], refs[-pieces:]
    each = len(blocks) * 8 // pieces if pieces > 1 else sends[0].shape[1]
    first = lax.axis_index("c") == 0
    sub = lax.broadcasted_iota(jnp.int32, (8, 128), 0)
    for n, (row, col) in enumerate(blocks):
        part = lax.dot_general(units[row][...], units[col][...], NT, preferred_element_type=f32)
        for zl in range(4):
            for y in range(4):
                at = (zl * 4 + y) * 16
                for cb in range(2):
                    a = part[at:at + 8, cb * 128:(cb + 1) * 128]
                    b = part[at + 8:at + 16, cb * 128:(cb + 1) * 128]
                    c0 = jnp.where(sub < 4, a, pltpu.roll(b, 4, 0))
                    c1 = jnp.where(sub < 4, pltpu.roll(a, 4, 0), b)
                    keep_ref[y, n * 8 + zl * 2 + cb] = jnp.where(first, c0, c1)
                    tile = n * 8 + zl * 2 + cb
                    sends[tile // each][y, tile % each] = jnp.where(first, c1, c0)
    if vectors:
        spread_ref, mean_ref = vectors[:2]
        end = len(blocks) * 8
        for y in range(4):
            for ref, own, other in ((keep_ref, 1, 2), (sends[0], 2, 1)):
                ref[y, end] = spread_ref[...]
                ref[y, end + own] = mean_ref[...]
                ref[y, end + other] = jnp.zeros((8, 128), f32)


def by_turn(early_ref, early_other_ref, late_ref, *refs):
    others, outs = refs[:-4], refs[-4:]
    y = lax.axis_index("y")
    start = early_ref.shape[1]
    each = late_ref.shape[1] // len(others)
    for turn, ref in enumerate(outs):
        to = (y + turn) % 4
        ref[:start] = early_ref[to] + early_other_ref[to]
        for n, other in enumerate(others):
            ref[start + n * each:start + (n + 1) * each] = late_ref[to, n * each:(n + 1) * each] + other[to]


def add(*refs):
    refs[-1][...] = refs[0][...] + refs[1][...]


def regroup(*refs):
    last, out_ref = refs[-2:]
    for q, blocks in enumerate(PARTS):
        turns = refs[0:4] if q < 2 else [last.at[y] for y in range(4)]
        start = len(PARTS[0]) * 8 if q == 1 else 0
        for n, (row, col) in enumerate(blocks):
            for zl in range(4):
                at, to = start + n * 8 + zl * 2, zl * 8 + col * 2
                a, b, c, d = [ref[at:at + 2] for ref in turns]
                out_ref[row, to:to + 2] = (a + b) + (c + d)
    end = len(PARTS[-1]) * 8
    spread = (last[0, end] + last[1, end]) + (last[2, end] + last[3, end])
    for x in range(4):
        out_ref[x, 32] = spread
        for y in range(4):
            out_ref[x, 33 + 2 * y:35 + 2 * y] = last[y, end + 1:end + 3]


def between(shift_ref, select):
    wide = jnp.concatenate([shift_ref[cb] for cb in range(8)], axis=1)
    rows = [
        lax.dot_general(one_hot, shift_ref[block], NT, precision=HI, preferred_element_type=f32)
        for block, one_hot in select
    ]
    rows = jnp.concatenate(rows, axis=0) if len(rows) > 1 else rows[0]
    return jnp.dot(rows, wide, precision=HI, preferred_element_type=f32)


def fold(part_ref, out_ref, shift_ref):
    x, y, c = lax.axis_index("x"), lax.axis_index("y"), lax.axis_index("c")
    sub = lax.broadcasted_iota(jnp.int32, (8, 128), 0)
    lane = lax.broadcasted_iota(jnp.int32, (8, 128), 1)

    def summed(t):
        return (part_ref[0, t] + part_ref[1, t]) + (part_ref[2, t] + part_ref[3, t])

    mean = summed(33)
    for k in range(1, 8):
        mean = mean + summed(33 + k)
    mean = mean * f32(1.0 / 32)
    spread = summed(32)
    for k in range(8):
        for p in range(4):
            shift = part_ref[p, 33 + k] - mean
            spread = spread + shift * shift * f32(TILE)
            for cb in range(8):
                shift_ref[cb, k * 4 + p:k * 4 + p + 1, :] = shift[cb:cb + 1]
    select = []
    for zl in range(4):
        want = (zl % 2) * 64 + y * 16 + (sub // 4) * 8 + c * 4 + sub % 4
        select.append((2 * x + zl // 2, jnp.where(lane == want, f32(1), f32(0))))
    extra = between(shift_ref, select) * f32(TILE)
    for zl in range(4):
        for k in range(4):
            a, b = [
                summed(zl * 8 + cb) + extra[zl * 8:zl * 8 + 8, cb * 128:(cb + 1) * 128] for cb in (2 * k, 2 * k + 1)
            ]
            out_ref[zl * 2, k] = jnp.where(sub < 4, a, pltpu.roll(b, 4, 0))
            out_ref[zl * 2 + 1, k] = jnp.where(sub < 4, pltpu.roll(a, 4, 0), b)
        for zh in range(2):
            out_ref[zl * 2 + zh, 4] = spread
            out_ref[zl * 2 + zh, 5] = mean


def finish(part_ref, out_ref, shift_ref):
    first_row = lax.axis_index(AXES) * 4
    sub = lax.broadcasted_iota(jnp.int32, (8, 128), 0)
    lane = lax.broadcasted_iota(jnp.int32, (8, 128), 1)

    def summed(t):
        s = part_ref[0, t]
        for p in range(1, 8):
            s = s + part_ref[p, t]
        return s

    mean = summed(5) * f32(1.0 / 8)
    spread = summed(4)
    for p in range(8):
        shift = part_ref[p, 5] - mean
        spread = spread + shift * shift * f32(32 * TILE)
        for cb in range(8):
            shift_ref[cb, p:p + 1, :] = shift[cb:cb + 1]
    one_hot = jnp.where(lane == first_row % 128 + sub % 4, f32(1), f32(0))
    extra = between(shift_ref, [(first_row // 128, one_hot)]) * f32(32 * TILE)
    scale = 1.0 / jnp.sqrt(spread + 1e-06)
    flat = sub * 128 + lane
    own = jnp.zeros((8, 128), f32)
    for i in range(4):
        value = jnp.sum(jnp.where(flat == first_row + i, scale, 0.0))
        own = jnp.where((sub & 3) == i, value, own)
    for k in range(4):
        at, to = 2 * k * 128, (2 * k + 1) * 128
        cols = jnp.where(sub < 4, scale[2 * k:2 * k + 1, :], scale[2 * k + 1:2 * k + 2, :])
        more = jnp.where(sub < 4, extra[:, at:to], extra[:, to:to + 128])
        tile = (summed(k) + more) * cols * own
        out_ref[:, at:to] = tile[0:4]
        out_ref[:, to:to + 128] = tile[4:8]


def local(images):
    shape = jax.ShapeDtypeStruct
    vmem = pl.BlockSpec(memory_space=pltpu.VMEM)
    anywhere = pl.BlockSpec(memory_space=pl.ANY)
    params = pltpu.CompilerParams(vmem_limit_bytes=48 * 1024 * 1024)
    by_group = images.reshape(4, 2048, 128)
    by_eighth = images.reshape(8, 1024, 128)
    up = [(i, i + 1) for i in range(15)]
    down = [(j, i) for i, j in up]
    edge_shape = [shape((256, 128), f32)] * 2

    def unit_shape(count):
        return [shape((count, 1024), jnp.bfloat16), shape((1, count), f32), shape((1, count), f32)]

    def swap(axes, ahead, back):
        return lax.ppermute(ahead, axes, up), lax.ppermute(back, axes, down)

    left, right = pl.pallas_call(
        survey,
        grid=(4,),
        in_specs=[pl.BlockSpec((4, 512, 128), lambda i: (0, i, 0))],
        out_specs=[pl.BlockSpec((64, 128), lambda i: (i, 0))] * 2,
        out_shape=edge_shape,
        compiler_params=pltpu.CompilerParams(vmem_limit_bytes=60 * 1024 * 1024),
    )(by_group)
    edges = swap(GY, right, left)
    weights = pl.pallas_call(
        build_weights,
        in_specs=[anywhere],
        out_specs=vmem,
        out_shape=shape((8, 256, 128), f32),
        compiler_params=params,
    )(left)

    def smooth_rows(start, count, order):
        top, bot = pl.pallas_call(
            functools.partial(row_pass, start, count),
            grid=(1,),
            in_specs=[pl.BlockSpec((count, 1024, 128), lambda i: (start // count, 0, 0))] + [vmem] * 3 + [anywhere],
            out_specs=[vmem] * 2,
            out_shape=[shape((4, 128 * count, 128), f32)] * 2,
            compiler_params=params,
        )(by_eighth, *edges, weights, order)
        above, below = swap(GX, bot, top)
        return above, top, bot, below

    def columns(sources, order):
        count = sources[0].shape[1]
        return pl.pallas_call(
            column_pass,
            in_specs=[vmem] * 4 + [anywhere] * len(order),
            out_specs=[vmem] * 3,
            out_shape=unit_shape(count),
            scratch_shapes=[pltpu.VMEM((count, 128), f32)] * 2,
            compiler_params=params,
        )(*sources, *order)

    def multiply(blocks, pieces, *operands):
        tiles = len(blocks) * 8 + (3 if len(operands) > 4 else 0)
        keep, *send = pl.pallas_call(
            functools.partial(gram, blocks, pieces),
            in_specs=([vmem] * 6 + [anywhere] * 4)[:len(operands)],
            out_specs=[vmem] * (1 + pieces),
            out_shape=[shape((4, tiles, 8, 128), f32)] + [shape((4, tiles // pieces, 8, 128), f32)] * pieces,
            compiler_params=params,
        )(*operands)
        return [keep] + [lax.ppermute(piece, "c", [(0, 1), (1, 0)]) for piece in send]

    chunks = []
    for start in (0, 2, 4, 6):
        chunks.append(smooth_rows(start, 2, chunks[-1][1] if chunks else left))
    results = [columns(chunks[0], [chunks[3][1]])]
    results.append(columns(chunks[1], [results[0][0]]))
    early = multiply(PARTS[0], 1, *[result[0] for result in results])
    results.append(columns(chunks[2], [early[0]]))
    late = multiply(PARTS[1], 4, *[result[0] for result in results])
    turns = pl.pallas_call(
        by_turn,
        in_specs=[vmem] * (3 + 4),
        out_specs=[vmem] * 4,
        out_shape=[shape((56, 8, 128), f32)] * 4,
        compiler_params=params,
    )(*early, *late)
    moved = [lax.ppermute(turns[k], "y", [(i, (i + k) % 4) for i in range(4)]) for k in range(1, 4)]
    results.append(columns(chunks[3], [turns[0]]))
    units, spreads, means = zip(*results)
    vectors = [jnp.concatenate(v, axis=1).reshape(8, 128) for v in (spreads, means)]
    keep, other = multiply(PARTS[2], 1, *units, *vectors, *moved)
    last = pl.pallas_call(
        add,
        in_specs=[vmem] * 2,
        out_specs=vmem,
        out_shape=shape(keep.shape, f32),
        compiler_params=params,
    )(keep, other)
    parts = [turns[0]] + moved + [lax.all_to_all(last, "y", 0, 0, tiled=True)]

    part = pl.pallas_call(
        regroup,
        in_specs=[vmem] * 5,
        out_specs=vmem,
        out_shape=shape((4, 41, 8, 128), f32),
        compiler_params=params,
    )(*parts)
    part = lax.all_to_all(part, "x", 0, 0, tiled=True)
    part = pl.pallas_call(
        fold,
        in_specs=[vmem],
        out_specs=vmem,
        out_shape=shape((8, 6, 8, 128), f32),
        scratch_shapes=[pltpu.VMEM((8, 32, 128), f32)],
        compiler_params=params,
    )(part)
    part = lax.all_to_all(part, ("zl", "zh"), 0, 0, tiled=True)
    return pl.pallas_call(
        finish,
        in_specs=[vmem],
        out_specs=vmem,
        out_shape=shape((4, 1024), f32),
        scratch_shapes=[pltpu.VMEM((8, 8, 128), f32)],
        compiler_params=params,
    )(part)


def solution(mesh):
    fine = Mesh(mesh.devices.reshape(4, 4, 4, 2, 2), AXES)
    return jax.shard_map(
        local,
        mesh=fine,
        in_specs=(P(None, GX, GY),),
        out_specs=P(AXES, None),
        check_vma=False,
    )
```

```python
import functools
import math

import jax
import jax.numpy as jnp
from jax import lax
from jax.experimental import pallas as pl
from jax.experimental.pallas import tpu as pltpu
from jax.sharding import Mesh, PartitionSpec as P

f32 = jnp.float32
HI = lax.Precision.HIGHEST
NT = (((1,), (1,)), ((), ()))
TILE = 8 * 128
PARTS = (
    ((0, 0), (0, 1), (1, 0), (1, 1)),
    ((2, 0), (2, 1), (0, 2)),
    ((3, 0), (3, 1), (3, 2), (3, 3), (0, 3), (1, 3), (2, 3), (2, 2), (1, 2)),
)
GX, GY = ("x", "zl"), ("y", "zh", "c")
AXES = GX + GY


def stencil_taps():
    raw = [math.exp(-k * k / 4.5) for k in range(-4, 5)]
    total = sum(raw)
    return [value / total for value in raw]


TAPS = stencil_taps()


def survey(x_ref, left_ref, right_ref):
    lane = lax.broadcasted_iota(jnp.int32, (64, 128), 1)
    left = jnp.zeros((64, 128), f32)
    right = jnp.zeros((64, 128), f32)
    for g in range(4):
        for r in range(8):
            row = x_ref[g, pl.ds(r, 64, stride=8), :]
            slot = g * 32 + r * 4
            after = (slot + 4) % 128
            turned = pltpu.roll(row, after, 1) if after else row
            right = jnp.where((lane >= slot) & (lane < slot + 4), turned, right)
            left = jnp.where((lane >= after) & (lane < after + 4), turned, left)
    left_ref[...] = pltpu.roll(left, 124, 1)
    right_ref[...] = right


def build_weights(order_ref, w_ref):
    at = lax.broadcasted_iota(jnp.int32, (128, 128), 0)
    col = lax.broadcasted_iota(jnp.int32, (128, 128), 1)

    def taps(distance):
        value = jnp.zeros((128, 128), f32)
        for k in range(5):
            value = jnp.where(distance == k, f32(TAPS[4 + k]), value)
        return value

    band = taps(jnp.abs(at - col))
    halo = taps(jnp.abs(at % 4 + jnp.where(at < 32, -4, 128) - col))
    for r in range(8):
        w_ref[r, 0:128] = band
        w_ref[r, 128:256] = jnp.where((at < 64) & (at % 32 // 4 == r), halo, 0.0)


def halo_lanes(g, left, right):
    lane = lax.broadcasted_iota(jnp.int32, left.shape, 1)
    left = pltpu.roll(left, (128 - 32 * g) % 128, 1) if g else left
    right = pltpu.roll(right, (160 - 32 * g) % 128, 1) if g != 1 else right
    return jnp.where(lane < 32, left, jnp.where(lane < 64, right, 0.0))


def smooth_row(row, halo, w):
    wide = jnp.concatenate([row, halo], axis=1)
    return jnp.dot(wide, w, precision=HI, preferred_element_type=f32)


def row_pass(start, count, x_ref, left_ref, right_ref, w_ref, order_ref, top_ref, bot_ref):
    halo = halo_lanes(start // 2, left_ref[...], right_ref[...])
    for r in range(8):
        row = jnp.concatenate([x_ref[part, pl.ds(r, 128, stride=8), :] for part in range(count)], axis=0)
        smooth = smooth_row(row, halo, w_ref[r])
        if r < 4:
            top_ref[r] = smooth
        else:
            bot_ref[r - 4] = smooth


def to_lanes(squares, level):
    ones = jnp.ones((8, 128), f32)
    pick = jnp.where(lax.broadcasted_iota(jnp.int32, (8, 128), 1) == 0, f32(1), f32(0))
    spread = lax.dot_general(ones, squares, NT, precision=HI, preferred_element_type=f32)
    mean = lax.dot_general(pick, level, NT, precision=HI, preferred_element_type=f32)
    return spread[0:1], mean[0:1]


def smooth_down(rows):
    smooth = []
    for r in range(8):
        v = rows[r + 4] * TAPS[4]
        for k in range(1, 5):
            v = v + (rows[r + 4 - k] + rows[r + 4 + k]) * TAPS[4 + k]
        smooth.append(v)
    return smooth


def column_pass(above_ref, top_ref, bot_ref, below_ref, *refs):
    u_ref, spread_ref, mean_ref, square_ref, level_ref = refs[-5:]

    def step(s, carry):
        at = pl.ds(pl.multiple_of(s * 16, 16), 16)
        smooth = smooth_down([ref[i, at, :] for ref in (above_ref, top_ref, bot_ref, below_ref) for i in range(4)])
        total = ((smooth[0] + smooth[1]) + (smooth[2] + smooth[3])) + ((smooth[4] + smooth[5]) + (smooth[6] + smooth[7]))
        mean = jnp.sum(total, axis=1, keepdims=True) * f32(1.0 / TILE)
        acc = jnp.zeros((16, 128), f32)
        for r in range(8):
            centered = smooth[r] - mean
            acc = acc + centered * centered
            u_ref[at, r * 128:(r + 1) * 128] = centered.astype(jnp.bfloat16)
        square_ref[at, :] = acc
        level_ref[at, :] = jnp.broadcast_to(mean, (16, 128))
        return carry

    lax.fori_loop(0, square_ref.shape[0] // 16, step, 0, unroll=4)
    spread_ref[...], mean_ref[...] = to_lanes(square_ref[...], level_ref[...])


def gram(blocks, pieces, *refs):
    count = 1 + max(a for a, b in blocks)
    units, refs = refs[:count], refs[count:]
    vectors, keep_ref, sends = refs[:-1 - pieces], refs[-1 - pieces], refs[-pieces:]
    each = len(blocks) * 8 // pieces if pieces > 1 else sends[0].shape[1]
    first = lax.axis_index("c") == 0
    sub = lax.broadcasted_iota(jnp.int32, (8, 128), 0)
    for n, (row, col) in enumerate(blocks):
        part = lax.dot_general(units[row][...], units[col][...], NT, preferred_element_type=f32)
        for zl in range(4):
            for y in range(4):
                at = (zl * 4 + y) * 16
                for cb in range(2):
                    a = part[at:at + 8, cb * 128:(cb + 1) * 128]
                    b = part[at + 8:at + 16, cb * 128:(cb + 1) * 128]
                    c0 = jnp.where(sub < 4, a, pltpu.roll(b, 4, 0))
                    c1 = jnp.where(sub < 4, pltpu.roll(a, 4, 0), b)
                    keep_ref[y, n * 8 + zl * 2 + cb] = jnp.where(first, c0, c1)
                    tile = n * 8 + zl * 2 + cb
                    sends[tile // each][y, tile % each] = jnp.where(first, c1, c0)
    if vectors:
        spread_ref, mean_ref = vectors[:2]
        end = len(blocks) * 8
        for y in range(4):
            for ref, own, other in ((keep_ref, 1, 2), (sends[0], 2, 1)):
                ref[y, end] = spread_ref[...]
                ref[y, end + own] = mean_ref[...]
                ref[y, end + other] = jnp.zeros((8, 128), f32)


def by_turn(early_ref, early_other_ref, late_ref, *refs):
    others, outs = refs[:-4], refs[-4:]
    y = lax.axis_index("y")
    start = early_ref.shape[1]
    each = late_ref.shape[1] // len(others)
    for turn, ref in enumerate(outs):
        to = (y + turn) % 4
        ref[:start] = early_ref[to] + early_other_ref[to]
        for n, other in enumerate(others):
            ref[start + n * each:start + (n + 1) * each] = late_ref[to, n * each:(n + 1) * each] + other[to]


def add(*refs):
    refs[-1][...] = refs[0][...] + refs[1][...]


def regroup(*refs):
    last, out_ref = refs[-2:]
    for q, blocks in enumerate(PARTS):
        turns = refs[0:4] if q < 2 else [last.at[y] for y in range(4)]
        start = len(PARTS[0]) * 8 if q == 1 else 0
        for n, (row, col) in enumerate(blocks):
            for zl in range(4):
                at, to = start + n * 8 + zl * 2, zl * 8 + col * 2
                a, b, c, d = [ref[at:at + 2] for ref in turns]
                out_ref[row, to:to + 2] = (a + b) + (c + d)
    end = len(PARTS[-1]) * 8
    spread = (last[0, end] + last[1, end]) + (last[2, end] + last[3, end])
    for x in range(4):
        out_ref[x, 32] = spread
        for y in range(4):
            out_ref[x, 33 + 2 * y:35 + 2 * y] = last[y, end + 1:end + 3]


def between(shift_ref, select):
    wide = jnp.concatenate([shift_ref[cb] for cb in range(8)], axis=1)
    rows = [
        lax.dot_general(one_hot, shift_ref[block], NT, precision=HI, preferred_element_type=f32)
        for block, one_hot in select
    ]
    rows = jnp.concatenate(rows, axis=0) if len(rows) > 1 else rows[0]
    return jnp.dot(rows, wide, precision=HI, preferred_element_type=f32)


def fold(part_ref, out_ref, shift_ref):
    x, y, c = lax.axis_index("x"), lax.axis_index("y"), lax.axis_index("c")
    sub = lax.broadcasted_iota(jnp.int32, (8, 128), 0)
    lane = lax.broadcasted_iota(jnp.int32, (8, 128), 1)

    def summed(t):
        return (part_ref[0, t] + part_ref[1, t]) + (part_ref[2, t] + part_ref[3, t])

    mean = summed(33)
    for k in range(1, 8):
        mean = mean + summed(33 + k)
    mean = mean * f32(1.0 / 32)
    spread = summed(32)
    for k in range(8):
        for p in range(4):
            shift = part_ref[p, 33 + k] - mean
            spread = spread + shift * shift * f32(TILE)
            for cb in range(8):
                shift_ref[cb, k * 4 + p:k * 4 + p + 1, :] = shift[cb:cb + 1]
    select = []
    for zl in range(4):
        want = (zl % 2) * 64 + y * 16 + (sub // 4) * 8 + c * 4 + sub % 4
        select.append((2 * x + zl // 2, jnp.where(lane == want, f32(1), f32(0))))
    extra = between(shift_ref, select) * f32(TILE)
    for zl in range(4):
        for k in range(4):
            a, b = [
                summed(zl * 8 + cb) + extra[zl * 8:zl * 8 + 8, cb * 128:(cb + 1) * 128] for cb in (2 * k, 2 * k + 1)
            ]
            out_ref[zl * 2, k] = jnp.where(sub < 4, a, pltpu.roll(b, 4, 0))
            out_ref[zl * 2 + 1, k] = jnp.where(sub < 4, pltpu.roll(a, 4, 0), b)
        for zh in range(2):
            out_ref[zl * 2 + zh, 4] = spread
            out_ref[zl * 2 + zh, 5] = mean


def finish(part_ref, out_ref, shift_ref):
    first_row = lax.axis_index(AXES) * 4
    sub = lax.broadcasted_iota(jnp.int32, (8, 128), 0)
    lane = lax.broadcasted_iota(jnp.int32, (8, 128), 1)

    def summed(t):
        s = part_ref[0, t]
        for p in range(1, 8):
            s = s + part_ref[p, t]
        return s

    mean = summed(5) * f32(1.0 / 8)
    spread = summed(4)
    for p in range(8):
        shift = part_ref[p, 5] - mean
        spread = spread + shift * shift * f32(32 * TILE)
        for cb in range(8):
            shift_ref[cb, p:p + 1, :] = shift[cb:cb + 1]
    one_hot = jnp.where(lane == first_row % 128 + sub % 4, f32(1), f32(0))
    extra = between(shift_ref, [(first_row // 128, one_hot)]) * f32(32 * TILE)
    scale = 1.0 / jnp.sqrt(spread + 1e-06)
    flat = sub * 128 + lane
    own = jnp.zeros((8, 128), f32)
    for i in range(4):
        value = jnp.sum(jnp.where(flat == first_row + i, scale, 0.0))
        own = jnp.where((sub & 3) == i, value, own)
    for k in range(4):
        at, to = 2 * k * 128, (2 * k + 1) * 128
        cols = jnp.where(sub < 4, scale[2 * k:2 * k + 1, :], scale[2 * k + 1:2 * k + 2, :])
        more = jnp.where(sub < 4, extra[:, at:to], extra[:, to:to + 128])
        tile = (summed(k) + more) * cols * own
        out_ref[:, at:to] = tile[0:4]
        out_ref[:, to:to + 128] = tile[4:8]


def local(images):
    shape = jax.ShapeDtypeStruct
    vmem = pl.BlockSpec(memory_space=pltpu.VMEM)
    anywhere = pl.BlockSpec(memory_space=pl.ANY)
    params = pltpu.CompilerParams(vmem_limit_bytes=48 * 1024 * 1024)
    by_group = images.reshape(4, 2048, 128)
    by_eighth = images.reshape(8, 1024, 128)
    up = [(i, i + 1) for i in range(15)]
    down = [(j, i) for i, j in up]
    edge_shape = [shape((256, 128), f32)] * 2

    def unit_shape(count):
        return [shape((count, 1024), jnp.bfloat16), shape((1, count), f32), shape((1, count), f32)]

    def swap(axes, ahead, back):
        return lax.ppermute(ahead, axes, up), lax.ppermute(back, axes, down)

    left, right = pl.pallas_call(
        survey,
        grid=(4,),
        in_specs=[pl.BlockSpec((4, 512, 128), lambda i: (0, i, 0))],
        out_specs=[pl.BlockSpec((64, 128), lambda i: (i, 0))] * 2,
        out_shape=edge_shape,
        compiler_params=pltpu.CompilerParams(vmem_limit_bytes=60 * 1024 * 1024),
    )(by_group)
    edges = swap(GY, right, left)
    weights = pl.pallas_call(
        build_weights,
        in_specs=[anywhere],
        out_specs=vmem,
        out_shape=shape((8, 256, 128), f32),
        compiler_params=params,
    )(left)

    def smooth_rows(start, count, order):
        top, bot = pl.pallas_call(
            functools.partial(row_pass, start, count),
            grid=(1,),
            in_specs=[pl.BlockSpec((count, 1024, 128), lambda i: (start // count, 0, 0))] + [vmem] * 3 + [anywhere],
            out_specs=[vmem] * 2,
            out_shape=[shape((4, 128 * count, 128), f32)] * 2,
            compiler_params=params,
        )(by_eighth, *edges, weights, order)
        above, below = swap(GX, bot, top)
        return above, top, bot, below

    def columns(sources, order):
        count = sources[0].shape[1]
        return pl.pallas_call(
            column_pass,
            in_specs=[vmem] * 4 + [anywhere] * len(order),
            out_specs=[vmem] * 3,
            out_shape=unit_shape(count),
            scratch_shapes=[pltpu.VMEM((count, 128), f32)] * 2,
            compiler_params=params,
        )(*sources, *order)

    def multiply(blocks, pieces, *operands):
        tiles = len(blocks) * 8 + (3 if len(operands) > 4 else 0)
        keep, *send = pl.pallas_call(
            functools.partial(gram, blocks, pieces),
            in_specs=([vmem] * 6 + [anywhere] * 4)[:len(operands)],
            out_specs=[vmem] * (1 + pieces),
            out_shape=[shape((4, tiles, 8, 128), f32)] + [shape((4, tiles // pieces, 8, 128), f32)] * pieces,
            compiler_params=params,
        )(*operands)
        return [keep] + [lax.ppermute(piece, "c", [(0, 1), (1, 0)]) for piece in send]

    chunks = []
    for start in (0, 2, 4, 6):
        chunks.append(smooth_rows(start, 2, chunks[-1][1] if chunks else left))
    results = [columns(chunks[0], [chunks[3][1]])]
    results.append(columns(chunks[1], [results[0][0]]))
    early = multiply(PARTS[0], 1, *[result[0] for result in results])
    results.append(columns(chunks[2], [early[0]]))
    late = multiply(PARTS[1], 4, *[result[0] for result in results])
    turns = pl.pallas_call(
        by_turn,
        in_specs=[vmem] * (3 + 4),
        out_specs=[vmem] * 4,
        out_shape=[shape((56, 8, 128), f32)] * 4,
        compiler_params=params,
    )(*early, *late)
    moved = [lax.ppermute(turns[k], "y", [(i, (i + k) % 4) for i in range(4)]) for k in range(1, 4)]
    results.append(columns(chunks[3], [turns[0]]))
    units, spreads, means = zip(*results)
    vectors = [jnp.concatenate(v, axis=1).reshape(8, 128) for v in (spreads, means)]
    keep, other = multiply(PARTS[2], 1, *units, *vectors, *moved)
    last = pl.pallas_call(
        add,
        in_specs=[vmem] * 2,
        out_specs=vmem,
        out_shape=shape(keep.shape, f32),
        compiler_params=params,
    )(keep, other)
    parts = [turns[0]] + moved + [lax.all_to_all(last, "y", 0, 0, tiled=True)]

    part = pl.pallas_call(
        regroup,
        in_specs=[vmem] * 5,
        out_specs=vmem,
        out_shape=shape((4, 41, 8, 128), f32),
        compiler_params=params,
    )(*parts)
    part = lax.all_to_all(part, "x", 0, 0, tiled=True)
    part = pl.pallas_call(
        fold,
        in_specs=[vmem],
        out_specs=vmem,
        out_shape=shape((8, 6, 8, 128), f32),
        scratch_shapes=[pltpu.VMEM((8, 32, 128), f32)],
        compiler_params=params,
    )(part)
    part = lax.all_to_all(part, ("zl", "zh"), 0, 0, tiled=True)
    return pl.pallas_call(
        finish,
        in_specs=[vmem],
        out_specs=vmem,
        out_shape=shape((4, 1024), f32),
        scratch_shapes=[pltpu.VMEM((8, 8, 128), f32)],
        compiler_params=params,
    )(part)


def solution(mesh):
    fine = Mesh(mesh.devices.reshape(4, 4, 4, 2, 2), AXES)
    return jax.shard_map(
        local,
        mesh=fine,
        in_specs=(P(None, GX, GY),),
        out_specs=P(AXES, None),
        check_vma=False,
    )
```
